32 devices in a mesh: grp: 2 (over x), ctx: 16 (over z, y, core).
Axes of the slice: x: 2, y: 2, z: 4, core: 2. Of those that a mesh axis runs over, the one named last changes fastest.
Arguments:
- hidden: bfloat16 [4, 7168], P('grp', 'ctx'), parts along dimension 0, may hold values from -6 to 6
- q_down: bfloat16 [7168, 1536], P('ctx'), may hold values from -0.0625 to 0.0625
- q_gain: float32 [1536], replicated, may hold values from 0.25 to 1.75
- q_up: bfloat16 [1536, 24576], P(None, 'ctx'), may hold values from -0.15625 to 0.15625
- w_uk: bfloat16 [128, 128, 512], P('ctx'), may hold values from -0.5 to 0.5
- kv_down: bfloat16 [7168, 576], P('ctx'), may hold values from -0.0625 to 0.0625
- kv_gain: float32 [512], replicated, may hold values from 3 to 8
- w_uv: bfloat16 [128, 512, 128], P('ctx'), may hold values from -0.25 to 0.25
- o_proj: bfloat16 [16384, 7168], P('ctx'), may hold values from -0.03125 to 0.03125
- cache: bfloat16 [4, 4096, 576], P('grp', 'ctx'), parts along dimension 0, may hold values from -40 to 40
- lengths: int32 [4], P('grp'), parts along dimension 0, may hold values from 2048 to 4096, as said below
- blocks: int32 [4, 32], P('grp'), parts along dimension 0, may hold values from 0 to 63, as said below
Outputs:
- attn_out: bfloat16 [4, 7168], P('grp', 'ctx'), parts along dimension 0
The draws below stay inside these ranges and needn't reach their ends.
There are 2 independent parts, one for each index of `grp`. The reference program is written for one: setup_inputs(seed, part) draws one part's arguments, and reference() takes and returns one part's arrays. A program takes and returns all parts, laid end to end along the dimension named above; an argument that names none is the same for every part. Nothing has to cross between parts.
Inputs may be any that keep to these rules, and one draw needn't show every extreme that they name: `lengths`: some row fills all 4096 slots. Each row names 32 different blocks, each starting below that row's length; the block of the row's last cached token is always among them.
All inputs are finite; a program needn't handle non-finite values.
Results may differ from the reference program's by a relative error of at most 0.02.
Values may be sent and summed in bfloat16 or wider, within the bound.
A program may use at most 192 MiB of HBM per device.

```python
import math
import jax
import jax.numpy as jnp
from jax import lax

D = 7168
H = 128
NOPE = 128
ROPE = 64
LAT = 512
VD = 128
QL = 1536
BLOCK = 64
TOPK = 32
ROWS = 2
CTX = 4096
QK = 192


def draw_common(key):
    folded = jax.random.fold_in(key, 7)
    key_len, key_score = jax.random.split(folded)
    count = CTX // BLOCK
    lens = jax.random.randint(key_len, (ROWS,), TOPK * BLOCK, CTX + 1).astype(jnp.int32)
    lens = lens.at[0].set(CTX)
    valid = (lens + BLOCK - 1) // BLOCK
    block_ids = jnp.arange(count, dtype=jnp.int32)
    score = jax.random.randint(key_score, (ROWS, count), 0, 65536).astype(jnp.int32) * count + block_ids[None, :]
    score = jnp.where(block_ids[None, :] == valid[:, None] - 1, score + (1 << 29), score)
    score = jnp.where(block_ids[None, :] < valid[:, None], score, -1 - block_ids[None, :])
    chosen = lax.top_k(score, TOPK)[1].astype(jnp.int32)
    return (lens, chosen)


def draw_lengths(key, part):
    return draw_common(key)[0]


def draw_blocks(key, part):
    return draw_common(key)[1]


def draw_cache(key, part):
    lens = draw_common(key)[0]
    key_val = jax.random.fold_in(jax.random.fold_in(key, 11), 0)
    key_sign = jax.random.fold_in(jax.random.fold_in(key, 11), 2)
    key_size = jax.random.fold_in(jax.random.fold_in(key, 11), 3)
    key_noise = jax.random.fold_in(jax.random.fold_in(key, 11), 4)
    values = jax.random.normal(key_val, (ROWS, CTX, LAT + ROPE), jnp.float32)
    values = jnp.clip(values, -6.0, 6.0)
    signs = jnp.where(jax.random.normal(key_sign, (ROWS, 1, LAT + ROPE), jnp.float32) < 0.0, -1.0, 1.0)
    sizes = jax.random.uniform(key_size, (ROWS, 1, LAT + ROPE), jnp.float32, 28.0, 40.0)
    strong = signs * sizes
    noise = jax.random.uniform(key_noise, (ROWS, 1, LAT + ROPE), jnp.float32, -1.5, 1.5)
    second = jnp.clip(strong + noise, -40.0, 40.0)
    slots = jnp.arange(CTX, dtype=jnp.int32)[None, :, None]
    last = lens[:, None, None]
    values = jnp.where(slots == last - 1, strong, values)
    values = jnp.where(slots == last - 2, second, values)
    return values.astype(jnp.bfloat16)


def block_scale(own_key, dims, pieces, smallest, top_value):
    level, own = 1.0, jax.random.fold_in(own_key, 6)
    for position, shards_of in pieces:
        heights = jnp.exp(jax.random.uniform(jax.random.fold_in(own, position), (shards_of,), jnp.float32, smallest / len(pieces), top_value / len(pieces)))
        level = level * jnp.repeat(heights, dims[position] // shards_of).reshape([-1 if axis == position else 1 for axis in range(len(dims))])
    return level


def scatter_about(own_key, extent, scale, most, cuts=(), held_as=jnp.bfloat16):
    values = scale * jax.random.normal(own_key, extent, jnp.float32)
    if cuts:
        values = values * block_scale(own_key, extent, cuts, -0.22, 0.18)
    return jnp.clip(values, -most, most).astype(held_as)


def setup_inputs(seed: int = 0, part: int = 0) -> dict:
    key_list = jax.random.split(jax.random.key(seed), 13)
    own_keys = jax.random.split(jax.random.fold_in(key_list[12], part), 13)
    return {
        "hidden": scatter_about(own_keys[0], (ROWS, D), 1.0, 6.0, ((1, 16),)),
        "q_down": scatter_about(key_list[1], (D, QL), D ** -0.5, 0.0625, ((0, 16),)),
        "q_gain": jnp.clip(1.0 + 0.15 * jax.random.normal(key_list[2], (QL,), jnp.float32), 0.25, 1.75),
        "q_up": scatter_about(key_list[3], (QL, H * QK), QL ** -0.5, 0.15625, ((1, 16),)),
        "w_uk": scatter_about(key_list[4], (H, NOPE, LAT), NOPE ** -0.5, 0.5, ((0, 16),)),
        "kv_down": scatter_about(key_list[5], (D, LAT + ROPE), D ** -0.5, 0.0625, ((0, 16),)),
        "kv_gain": jnp.clip(jnp.exp(jax.random.uniform(key_list[6], (LAT,), jnp.float32, math.log(3.0), math.log(8.0))), 3.0, 8.0),
        "w_uv": scatter_about(key_list[7], (H, LAT, VD), LAT ** -0.5, 0.25, ((0, 16),)),
        "o_proj": scatter_about(key_list[8], (H * VD, D), (2 * H * VD) ** -0.5, 0.03125, ((0, 16),)),
        "cache": draw_cache(jax.random.fold_in(jax.random.fold_in(key_list[12], part), 71), part),
        "lengths": draw_lengths(jax.random.fold_in(jax.random.fold_in(key_list[12], part), 71), part),
        "blocks": draw_blocks(jax.random.fold_in(jax.random.fold_in(key_list[12], part), 71), part),
    }


def rms_scale(values, gain):
    return values * lax.rsqrt(lax.optimization_barrier(jnp.mean(values * values, axis=-1, keepdims=True)) + 1e-06) * gain

def reference(hidden, q_down, q_gain, q_up, w_uk, kv_down, kv_gain, w_uv, o_proj, cache, lengths, blocks):
    q_low = jnp.dot(hidden, q_down, preferred_element_type=jnp.float32)
    kv_new = jnp.dot(hidden, kv_down, preferred_element_type=jnp.float32)
    q_normed = rms_scale(q_low, q_gain).astype(jnp.bfloat16)
    q_full = jnp.dot(q_normed, q_up, preferred_element_type=jnp.float32).astype(jnp.bfloat16)
    q_full = q_full.reshape(ROWS, H, NOPE + ROPE)
    q_lat = jnp.einsum('rhn,hnl->rhl', q_full[:, :, :NOPE].astype(jnp.float32), w_uk.astype(jnp.float32))
    query = jnp.concatenate([q_lat, q_full[:, :, NOPE:].astype(jnp.float32)], axis=-1).astype(jnp.bfloat16)
    lat_new = rms_scale(kv_new[:, :LAT], kv_gain)
    key_new = jnp.concatenate([lat_new, kv_new[:, LAT:]], axis=-1).astype(jnp.bfloat16)
    scale = (NOPE + ROPE) ** (-0.5)
    own = scale * jnp.einsum('rhc,rc->rh', query.astype(jnp.float32), key_new.astype(jnp.float32))
    slots = jnp.arange(CTX, dtype=jnp.int32)

    def one_row(args):
        query_row, cache_row, length, chosen, own_row, key_row = args
        used = jnp.any((slots // BLOCK)[None, :] == chosen[:, None], axis=0) & (slots < length)
        score = scale * jnp.dot(query_row, cache_row.T, preferred_element_type=jnp.float32)
        peak = jnp.maximum(lax.optimization_barrier(jnp.max(jnp.where(used[None, :], score, -1e+30), axis=1)), own_row)
        expo = jnp.where(used[None, :], jnp.exp(score - peak[:, None]), 0.0)
        own_w = jnp.exp(own_row - peak)
        denom = lax.optimization_barrier(jnp.sum(expo, axis=1)) + own_w
        weights = expo.astype(jnp.bfloat16)
        numer = jnp.dot(weights, cache_row[:, :LAT], preferred_element_type=jnp.float32)
        numer = numer + own_w[:, None] * key_row[None, :LAT].astype(jnp.float32)
        return (numer / denom[:, None]).astype(jnp.bfloat16)
    latent = lax.map(one_row, (query, cache, lengths, blocks, own, key_new))
    head_out = jnp.einsum('rhl,hlv->rhv', latent.astype(jnp.float32), w_uv.astype(jnp.float32))
    head_out = head_out.astype(jnp.bfloat16).reshape(ROWS, H * VD)
    return jnp.dot(head_out, o_proj, preferred_element_type=jnp.float32).astype(jnp.bfloat16)
```

```python
import functools
import math

import jax
import jax.numpy as jnp
from jax import lax
from jax.experimental import pallas as pl
from jax.experimental.pallas import tpu as pltpu
from jax.sharding import PartitionSpec as P

NOPE = 128
ROPE = 64
BLOCK = 64
LANES = 128
F32 = jnp.float32
BF16 = jnp.bfloat16
MESH = pl.DeviceIdType.MESH


def dot(a, b):
    return jnp.dot(a, b, preferred_element_type=F32)


def split3(value):
    high = value.astype(BF16).astype(F32)
    mid = (value - high).astype(BF16).astype(F32)
    return high, mid, value - high - mid


def kernel(
    n, rows, heads, lat, pad,
    lengths, blocks, hidden, q_gain, kv_gain,
    q_down, kv_down, q_up, w_uk, cache, w_uv, o_proj,
    out,
    v_qd, v_kd, v_qu, v_uk, v_ca, v_uv, v_op,
    s1, r1, g2, qf, qs, qall, s4, r4, s5, r5,
    load_sem, send_sem, recv_sem,
):
    me = lax.axis_index("ctx")
    ql = q_down.shape[1]
    kvw = kv_down.shape[1]
    kr = heads * rows
    head_width = NOPE + ROPE
    q_rows = q_up.shape[0]
    o_rows = o_proj.shape[0]
    scale = head_width ** (-0.5)

    loads = []

    def load(src, dst, parts=1):
        mine = []
        size = src.shape[0] // parts
        for part in range(parts):
            where = pl.ds(part * size, size)
            copy = pltpu.make_async_copy(src.at[where], dst.at[where], load_sem.at[len(loads)])
            copy.start()
            loads.append(copy)
            mine.append(copy)
        return mine

    l_qd = load(q_down, v_qd)
    l_kd = load(kv_down, v_kd)
    l_qu = load(q_up, v_qu, 4)
    l_uk = load(w_uk, v_uk)
    l_ca = load(cache, v_ca)
    l_uv = load(w_uv, v_uv)
    l_op = load(o_proj, v_op, 8)

    def arrive(copies):
        for copy in copies:
            copy.wait()

    barrier = pltpu.get_barrier_semaphore()

    def greet(k, _):
        pl.semaphore_signal(
            barrier, inc=1, device_id={"ctx": lax.rem(me + k, n)}, device_id_type=MESH
        )
        return 0

    lax.fori_loop(1, n, greet, 0)

    def remote(phase, src, dst, peer):
        return pltpu.make_async_remote_copy(
            src_ref=src, dst_ref=dst,
            send_sem=send_sem.at[phase, peer], recv_sem=recv_sem.at[phase, me],
            device_id={"ctx": peer}, device_id_type=MESH,
        )

    def send_all(phase, source, dst):
        def body(k, _):
            peer = lax.rem(me + k, n)
            remote(phase, source(peer), dst.at[me], peer).start()
            return 0

        lax.fori_loop(1, n, body, 0)

    def wait_all(phase, source, dst):
        def body(k, _):
            peer = lax.rem(me + k, n)
            pltpu.make_async_remote_copy(
                src_ref=source(peer), dst_ref=dst.at[peer],
                send_sem=send_sem.at[phase, peer], recv_sem=recv_sem.at[phase, peer],
                device_id={"ctx": peer}, device_id_type=MESH,
            ).wait()
            return 0

        lax.fori_loop(1, n, body, 0)

    q_chunks = ql // LANES
    kv_chunks = -(-kvw // LANES)
    chunks = q_chunks + kv_chunks
    s1[...] = jnp.zeros_like(s1)
    x = hidden[...]
    arrive(l_qd)
    q_part = dot(x, v_qd[...])
    arrive(l_kd)
    kv_part = dot(x, v_kd[...])
    for c in range(chunks):
        d, s = c % n, c // n
        where = pl.ds(s * rows, rows)
        if c < q_chunks:
            s1[d, where, :] = q_part[:, c * LANES:(c + 1) * LANES]
        else:
            begin = (c - q_chunks) * LANES
            width = min(LANES, kvw - begin)
            s1[d, where, :width] = kv_part[:, begin:begin + width]
    r1[me] = s1[me]
    pl.semaphore_wait(barrier, n - 1)
    send_all(0, lambda peer: s1.at[peer], r1)

    tokens = cache.shape[1]
    token = lax.broadcasted_iota(jnp.int32, (1, tokens), 1)
    position = me * tokens + token
    block_of = position // BLOCK
    used = []
    for r in range(rows):
        hit = block_of == blocks[r, 0]
        for k in range(1, blocks.shape[1]):
            hit = hit | (block_of == blocks[r, k])
        used.append(jnp.where(hit & (position < lengths[r]), 1.0, 0.0))
    used = jnp.concatenate(used, axis=1)
    row_of_token = lax.broadcasted_iota(jnp.int32, (n * pad, rows * tokens), 1) // tokens
    row_of_query = lax.broadcasted_iota(jnp.int32, (n * pad, rows * tokens), 0) % rows
    valid = (row_of_token == row_of_query) & (used > 0.5)
    if pad > kr:
        qs[...] = jnp.zeros_like(qs)

    wait_all(0, lambda peer: s1.at[peer], r1)
    g2[me] = jnp.sum(r1[...], axis=0)
    send_all(1, lambda peer: g2.at[me], g2)
    wait_all(1, lambda peer: g2.at[me], g2)

    def chunk(c):
        return g2[c % n, pl.ds((c // n) * rows, rows), :]

    q_low = jnp.concatenate([chunk(c) for c in range(q_chunks)], axis=1)
    kv_new = jnp.concatenate([chunk(c) for c in range(q_chunks, chunks)], axis=1)[:, :kvw]
    q_mean = jnp.sum(q_low * q_low, axis=1, keepdims=True) * (1.0 / ql)
    q_normed = (q_low * lax.rsqrt(q_mean + 1e-06) * q_gain[...]).astype(BF16)
    arrive(l_qu)
    qf[...] = dot(q_normed, v_qu[...]).astype(BF16).astype(F32)
    arrive(l_uk)
    for h in range(heads):
        nope = qf[:, h * head_width:h * head_width + NOPE].astype(BF16)
        where = pl.ds(h * rows, rows)
        qs[where, :lat] = dot(nope, v_uk[h])
        qs[where, lat:] = qf[:, h * head_width + NOPE:(h + 1) * head_width]
    query = qs[...].astype(BF16)
    qall[me] = query
    send_all(2, lambda peer: qall.at[me], qall)

    kv_lat = kv_new[:, :lat]
    kv_mean = jnp.sum(kv_lat * kv_lat, axis=1, keepdims=True) * (1.0 / lat)
    lat_new = kv_lat * lax.rsqrt(kv_mean + 1e-06) * kv_gain[...]
    key_new = jnp.concatenate([lat_new, kv_new[:, lat:]], axis=1).astype(BF16).astype(F32)
    own_row = lax.broadcasted_iota(jnp.int32, (pad, kvw), 0) % rows
    key_rows = jnp.broadcast_to(key_new[0:1], (pad, kvw))
    for r in range(1, rows):
        key_rows = jnp.where(own_row == r, jnp.broadcast_to(key_new[r:r + 1], (pad, kvw)), key_rows)
    own = scale * jnp.sum(query.astype(F32) * key_rows, axis=1, keepdims=True)

    arrive(l_ca)
    wait_all(2, lambda peer: qall.at[me], qall)
    q_mat = qall[...].reshape(n * pad, kvw)
    c_mat = v_ca[...].reshape(rows * tokens, kvw)
    score = scale * lax.dot_general(
        q_mat, c_mat, (((1,), (1,)), ((), ())), preferred_element_type=F32
    )
    peak = jnp.max(jnp.where(valid, score, -1e30), axis=1, keepdims=True)
    expo = jnp.where(valid, jnp.exp(score - peak), 0.0)
    total = jnp.sum(expo, axis=1, keepdims=True)
    numer = dot(expo.astype(BF16), c_mat[:, :lat])
    s4[:, :, :lat] = numer.astype(BF16).reshape(n, pad, lat)
    lane = lax.broadcasted_iota(jnp.int32, (n * pad, LANES), 1)
    stats = jnp.zeros((n * pad, LANES), F32)
    for place, piece in enumerate(split3(peak) + split3(total)):
        stats = jnp.where(lane == place, piece, stats)
    s4[:, :, lat:] = stats.astype(BF16).reshape(n, pad, LANES)
    send_all(3, lambda peer: s4.at[peer], r4)
    r4[me] = s4[me]
    wait_all(3, lambda peer: s4.at[peer], r4)

    got = r4[:, :, lat:].astype(F32)
    peaks = got[:, :, 0:1] + got[:, :, 1:2] + got[:, :, 2:3]
    totals = got[:, :, 3:4] + got[:, :, 4:5] + got[:, :, 5:6]
    top = jnp.maximum(jnp.max(peaks, axis=0), own)
    factor = jnp.exp(peaks - top[None])
    own_weight = jnp.exp(own - top)
    denom = jnp.sum(totals * factor, axis=0) + own_weight
    mixed = own_weight * key_rows[:, :lat]
    for d in range(n):
        mixed = mixed + factor[d] * r4[d, :, :lat].astype(F32)
    latent = (mixed / denom).astype(BF16).astype(F32)
    arrive(l_uv)
    head_out = jnp.concatenate(
        [dot(latent[h * rows:(h + 1) * rows].astype(BF16), v_uv[h]) for h in range(heads)], axis=1
    ).astype(BF16)

    arrive(l_op)
    width = out.shape[1]
    group = math.lcm(width, LANES)
    for g in range(n * width // group):
        part = dot(head_out, v_op[:, g * group:(g + 1) * group])
        for i in range(group // width):
            d = g * (group // width) + i
            s5[d] = part[:, i * width:(i + 1) * width]

            @pl.when(me != d)
            def _():
                remote(4, s5.at[d], r5.at[me], d).start()

    r5[me] = s5[me]
    wait_all(4, lambda peer: s5.at[peer], r5)
    out[...] = jnp.sum(r5[...], axis=0).astype(BF16)


def solution(mesh):
    n = mesh.shape["ctx"]

    def per_device(
        hidden, q_down, q_gain, q_up, w_uk, kv_down, kv_gain, w_uv, o_proj, cache, lengths, blocks
    ):
        rows = hidden.shape[0]
        heads, _, lat = w_uk.shape
        kvw = kv_down.shape[1]
        width = o_proj.shape[1] // n
        pad = -(-rows * heads // 16) * 16
        chunks = q_down.shape[1] // LANES + -(-kvw // LANES)
        held = -(-chunks // n) * rows
        vmem = pl.BlockSpec(memory_space=pltpu.VMEM)
        smem = pl.BlockSpec(memory_space=pltpu.SMEM)
        hbm = pl.BlockSpec(memory_space=pl.ANY)
        big = (q_down, kv_down, q_up, w_uk, cache, w_uv, o_proj)
        return pl.pallas_call(
            functools.partial(kernel, n, rows, heads, lat, pad),
            out_shape=jax.ShapeDtypeStruct((rows, width), BF16),
            in_specs=[smem, smem, vmem, vmem, vmem] + [hbm] * len(big),
            out_specs=vmem,
            scratch_shapes=[pltpu.VMEM(a.shape, a.dtype) for a in big] + [
                pltpu.VMEM((n, held, LANES), F32),
                pltpu.VMEM((n, held, LANES), F32),
                pltpu.VMEM((n, held, LANES), F32),
                pltpu.VMEM((rows, q_up.shape[1]), F32),
                pltpu.VMEM((pad, kvw), F32),
                pltpu.VMEM((n, pad, kvw), BF16),
                pltpu.VMEM((n, pad, lat + LANES), BF16),
                pltpu.VMEM((n, pad, lat + LANES), BF16),
                pltpu.VMEM((n, rows, width), F32),
                pltpu.VMEM((n, rows, width), F32),
                pltpu.SemaphoreType.DMA((17,)),
                pltpu.SemaphoreType.DMA((5, n)),
                pltpu.SemaphoreType.DMA((5, n)),
            ],
            compiler_params=pltpu.CompilerParams(
                collective_id=0, has_side_effects=True, vmem_limit_bytes=56 * 1024 * 1024
            ),
        )(lengths, blocks, hidden, q_gain[None], kv_gain[None], *big)

    placed = (
        P("grp", "ctx"),
        P("ctx", None),
        P(),
        P(None, "ctx"),
        P("ctx", None, None),
        P("ctx", None),
        P(),
        P("ctx", None, None),
        P("ctx", None),
        P("grp", "ctx", None),
        P("grp"),
        P("grp", None),
    )
    return jax.shard_map(
        per_device, mesh=mesh, in_specs=placed, out_specs=P("grp", "ctx"), check_vma=False
    )
```

```python
import functools
import math

import jax
import jax.numpy as jnp
from jax import lax
from jax.experimental import pallas as pl
from jax.experimental.pallas import tpu as pltpu
from jax.sharding import PartitionSpec as P

NOPE = 128
ROPE = 64
PAIR = 2
BLOCK = 64
LANES = 128
F32 = jnp.float32
BF16 = jnp.bfloat16
MESH = pl.DeviceIdType.MESH


def dot(a, b):
    return jnp.dot(a, b, preferred_element_type=F32)


def split3(value):
    high = value.astype(BF16).astype(F32)
    mid = (value - high).astype(BF16).astype(F32)
    return high, mid, value - high - mid


def kernel(
    n, rows, heads, lat, pad,
    lengths, blocks, hidden, q_gain, kv_gain,
    q_down, kv_down, q_up, w_uk, cache, w_uv, o_proj,
    out,
    v_qd, v_kd, v_qu, v_uk, v_ca, v_uv, v_op,
    s1, r1, g2, qf, qs, qall, s4, r4, s5, r5,
    load_sem, pair_sem, send_sem, recv_sem,
):
    me = lax.axis_index("ctx")
    ql = q_down.shape[1]
    kvw = kv_down.shape[1]
    kr = heads * rows
    head_width = NOPE + ROPE
    q_rows = q_up.shape[0]
    o_rows = o_proj.shape[0]
    scale = head_width ** (-0.5)

    loads = []

    def load(src, dst, parts=1):
        mine = []
        size = src.shape[0] // parts
        for part in range(parts):
            where = pl.ds(part * size, size)
            copy = pltpu.make_async_copy(src.at[where], dst.at[where], load_sem.at[len(loads)])
            copy.start()
            loads.append(copy)
            mine.append(copy)
        return mine

    l_qd = load(q_down, v_qd)
    l_kd = load(kv_down, v_kd)
    l_qu = load(q_up, v_qu, 4)
    l_uk = load(w_uk, v_uk)
    core = lax.rem(me, PAIR)
    l_ca = load(cache, v_ca.at[core])
    l_uv = load(w_uv, v_uv)
    l_op = load(o_proj, v_op, 8)

    def arrive(copies):
        for copy in copies:
            copy.wait()

    barrier = pltpu.get_barrier_semaphore()

    def greet(k, _):
        pl.semaphore_signal(
            barrier, inc=1, device_id={"ctx": lax.rem(me + k, n)}, device_id_type=MESH
        )
        return 0

    lax.fori_loop(1, n, greet, 0)

    everyone = (n, me, lambda index: index)
    alike = (n // PAIR, me // PAIR, lambda index: index * PAIR + core)

    def remote(phase, src, dst, peer, slot, device):
        return pltpu.make_async_remote_copy(
            src_ref=src, dst_ref=dst,
            send_sem=send_sem.at[phase, peer], recv_sem=recv_sem.at[phase, slot],
            device_id={"ctx": device}, device_id_type=MESH,
        )

    def send_all(phase, team, source, dst):
        size, mine, device = team

        def body(k, _):
            peer = lax.rem(mine + k, size)
            remote(phase, source(peer), dst.at[mine], peer, mine, device(peer)).start()
            return 0

        lax.fori_loop(1, size, body, 0)

    def wait_all(phase, team, source, dst):
        size, mine, device = team

        def body(k, _):
            peer = lax.rem(mine + k, size)
            remote(phase, source(peer), dst.at[peer], peer, peer, device(peer)).wait()
            return 0

        lax.fori_loop(1, size, body, 0)

    q_chunks = ql // LANES
    kv_chunks = -(-kvw // LANES)
    chunks = q_chunks + kv_chunks
    s1[...] = jnp.zeros_like(s1)
    x = hidden[...]
    arrive(l_qd)
    q_part = dot(x, v_qd[...])
    arrive(l_kd)
    kv_part = dot(x, v_kd[...])
    for c in range(chunks):
        d, s = c % n, c // n
        where = pl.ds(s * rows, rows)
        if c < q_chunks:
            s1[d, where, :] = q_part[:, c * LANES:(c + 1) * LANES]
        else:
            begin = (c - q_chunks) * LANES
            width = min(LANES, kvw - begin)
            s1[d, where, :width] = kv_part[:, begin:begin + width]
    r1[me] = s1[me]
    pl.semaphore_wait(barrier, n - 1)
    send_all(0, everyone, lambda peer: s1.at[peer], r1)
    partner = me + 1 - 2 * core
    share = pltpu.make_async_remote_copy(
        src_ref=cache, dst_ref=v_ca.at[core], send_sem=pair_sem.at[0], recv_sem=pair_sem.at[1],
        device_id={"ctx": partner}, device_id_type=MESH,
    )
    share.start()

    tokens = cache.shape[2]
    token = lax.broadcasted_iota(jnp.int32, (1, PAIR * tokens), 1)
    position = (me - core) * tokens + token
    block_of = position // BLOCK
    used = []
    for r in range(rows):
        hit = block_of == blocks[r, 0]
        for k in range(1, blocks.shape[1]):
            hit = hit | (block_of == blocks[r, k])
        used.append(jnp.where(hit & (position < lengths[r]), 1.0, 0.0))
    used = jnp.concatenate(used, axis=1)
    shape = (n // PAIR * pad, rows * PAIR * tokens)
    row_of_token = lax.broadcasted_iota(jnp.int32, shape, 1) // (PAIR * tokens)
    row_of_query = lax.broadcasted_iota(jnp.int32, shape, 0) % rows
    valid = (row_of_token == row_of_query) & (used > 0.5)
    if pad > kr:
        qs[...] = jnp.zeros_like(qs)

    wait_all(0, everyone, lambda peer: s1.at[peer], r1)
    g2[me] = jnp.sum(r1[...], axis=0)
    send_all(1, everyone, lambda peer: g2.at[me], g2)
    wait_all(1, everyone, lambda peer: g2.at[me], g2)

    def chunk(c):
        return g2[c % n, pl.ds((c // n) * rows, rows), :]

    q_low = jnp.concatenate([chunk(c) for c in range(q_chunks)], axis=1)
    kv_new = jnp.concatenate([chunk(c) for c in range(q_chunks, chunks)], axis=1)[:, :kvw]
    q_mean = jnp.sum(q_low * q_low, axis=1, keepdims=True) * (1.0 / ql)
    gain = jnp.concatenate([q_gain[c:c + 1, :] for c in range(q_chunks)], axis=1)
    q_normed = (q_low * lax.rsqrt(q_mean + 1e-06) * gain).astype(BF16)
    arrive(l_qu)
    qf[...] = dot(q_normed, v_qu[...]).astype(BF16).astype(F32)
    arrive(l_uk)
    for h in range(heads):
        nope = qf[:, h * head_width:h * head_width + NOPE].astype(BF16)
        where = pl.ds(h * rows, rows)
        qs[where, :lat] = dot(nope, v_uk[h])
        qs[where, lat:] = qf[:, h * head_width + NOPE:(h + 1) * head_width]
    query = qs[...].astype(BF16)
    qall[me // PAIR] = query
    send_all(2, alike, lambda peer: qall.at[me // PAIR], qall)

    kv_lat = kv_new[:, :lat]
    kv_mean = jnp.sum(kv_lat * kv_lat, axis=1, keepdims=True) * (1.0 / lat)
    lat_new = kv_lat * lax.rsqrt(kv_mean + 1e-06) * kv_gain[...]
    key_new = jnp.concatenate([lat_new, kv_new[:, lat:]], axis=1).astype(BF16).astype(F32)
    own_row = lax.broadcasted_iota(jnp.int32, (pad, kvw), 0) % rows
    key_rows = jnp.broadcast_to(key_new[0:1], (pad, kvw))
    for r in range(1, rows):
        key_rows = jnp.where(own_row == r, jnp.broadcast_to(key_new[r:r + 1], (pad, kvw)), key_rows)
    own = scale * jnp.sum(query.astype(F32) * key_rows, axis=1, keepdims=True)

    arrive(l_ca)
    pltpu.make_async_remote_copy(
        src_ref=cache, dst_ref=v_ca.at[1 - core], send_sem=pair_sem.at[0], recv_sem=pair_sem.at[1],
        device_id={"ctx": partner}, device_id_type=MESH,
    ).wait()
    wait_all(2, alike, lambda peer: qall.at[me // PAIR], qall)
    q_mat = qall[...].reshape(n // PAIR * pad, kvw)
    parts = [(half, r) for r in range(rows) for half in range(PAIR)]
    score = scale * jnp.concatenate([dot(q_mat, v_ca[half, r]) for half, r in parts], axis=1)
    peak = jnp.max(jnp.where(valid, score, -1e30), axis=1, keepdims=True)
    expo = jnp.where(valid, jnp.exp(score - peak), 0.0)
    total = jnp.sum(expo, axis=1, keepdims=True)
    weights = expo.astype(BF16)
    numer = jnp.zeros((n // PAIR * pad, lat), F32)
    for place, (half, r) in enumerate(parts):
        numer = numer + lax.dot_general(
            weights[:, place * tokens:(place + 1) * tokens], v_ca[half, r, :lat, :],
            (((1,), (1,)), ((), ())), preferred_element_type=F32,
        )
    s4[:, :, :lat] = numer.astype(BF16).reshape(n // PAIR, pad, lat)
    lane = lax.broadcasted_iota(jnp.int32, (n // PAIR * pad, LANES), 1)
    stats = jnp.zeros((n // PAIR * pad, LANES), F32)
    for place, piece in enumerate(split3(peak) + split3(total)):
        stats = jnp.where(lane == place, piece, stats)
    s4[:, :, lat:] = stats.astype(BF16).reshape(n // PAIR, pad, LANES)
    send_all(3, alike, lambda peer: s4.at[peer], r4)
    r4[me // PAIR] = s4[me // PAIR]
    wait_all(3, alike, lambda peer: s4.at[peer], r4)

    got = r4[:, :, lat:].astype(F32)
    peaks = got[:, :, 0:1] + got[:, :, 1:2] + got[:, :, 2:3]
    totals = got[:, :, 3:4] + got[:, :, 4:5] + got[:, :, 5:6]
    top = jnp.maximum(jnp.max(peaks, axis=0), own)
    factor = jnp.exp(peaks - top[None])
    own_weight = jnp.exp(own - top)
    denom = jnp.sum(totals * factor, axis=0) + own_weight
    mixed = own_weight * key_rows[:, :lat]
    for d in range(n // PAIR):
        mixed = mixed + factor[d] * r4[d, :, :lat].astype(F32)
    latent = (mixed / denom).astype(BF16).astype(F32)
    arrive(l_uv)
    head_out = jnp.concatenate(
        [dot(latent[h * rows:(h + 1) * rows].astype(BF16), v_uv[h]) for h in range(heads)], axis=1
    ).astype(BF16)

    arrive(l_op)
    width = out.shape[1]
    group = math.lcm(width, 2 * LANES)
    for g in range(n * width // group):
        part = dot(head_out, v_op[:, g * group:(g + 1) * group])
        for i in range(group // width):
            d = g * (group // width) + i
            s5[d] = part[:, i * width:(i + 1) * width]

            @pl.when(me != d)
            def _():
                remote(4, s5.at[d], r5.at[me], d, me, d).start()

    r5[me] = s5[me]
    wait_all(4, everyone, lambda peer: s5.at[peer], r5)
    out[...] = jnp.sum(r5[...], axis=0).astype(BF16)


def solution(mesh):
    n = mesh.shape["ctx"]

    def per_device(
        hidden, q_down, q_gain, q_up, w_uk, kv_down, kv_gain, w_uv, o_proj, cache, lengths, blocks
    ):
        rows = hidden.shape[0]
        heads, _, lat = w_uk.shape
        kvw = kv_down.shape[1]
        width = o_proj.shape[1] // n
        pad = -(-rows * heads // 16) * 16
        chunks = q_down.shape[1] // LANES + -(-kvw // LANES)
        held = -(-chunks // n) * rows
        vmem = pl.BlockSpec(memory_space=pltpu.VMEM)
        smem = pl.BlockSpec(memory_space=pltpu.SMEM)
        hbm = pl.BlockSpec(memory_space=pl.ANY)
        cache = jnp.swapaxes(cache, 1, 2)
        big = (q_down, kv_down, q_up, w_uk, cache, w_uv, o_proj)
        held_in = [a.shape for a in big]
        held_in[4] = (PAIR,) + cache.shape
        return pl.pallas_call(
            functools.partial(kernel, n, rows, heads, lat, pad),
            out_shape=jax.ShapeDtypeStruct((rows, width), BF16),
            in_specs=[smem, smem, vmem, vmem, vmem] + [hbm] * len(big),
            out_specs=vmem,
            scratch_shapes=[pltpu.VMEM(shape, BF16) for shape in held_in] + [
                pltpu.VMEM((n, held, LANES), F32),
                pltpu.VMEM((n, held, LANES), F32),
                pltpu.VMEM((n, held, LANES), F32),
                pltpu.VMEM((rows, q_up.shape[1]), F32),
                pltpu.VMEM((pad, kvw), F32),
                pltpu.VMEM((n // PAIR, pad, kvw), BF16),
                pltpu.VMEM((n // PAIR, pad, lat + LANES), BF16),
                pltpu.VMEM((n // PAIR, pad, lat + LANES), BF16),
                pltpu.VMEM((n, rows, width), F32),
                pltpu.VMEM((n, rows, width), F32),
                pltpu.SemaphoreType.DMA((17,)),
                pltpu.SemaphoreType.DMA((2,)),
                pltpu.SemaphoreType.DMA((5, n)),
                pltpu.SemaphoreType.DMA((5, n)),
            ],
            compiler_params=pltpu.CompilerParams(
                collective_id=0, has_side_effects=True, vmem_limit_bytes=56 * 1024 * 1024
            ),
        )(lengths, blocks, hidden, q_gain.reshape(-1, LANES), kv_gain[None], *big)

    placed = (
        P("grp", "ctx"),
        P("ctx", None),
        P(),
        P(None, "ctx"),
        P("ctx", None, None),
        P("ctx", None),
        P(),
        P("ctx", None, None),
        P("ctx", None),
        P("grp", "ctx", None),
        P("grp"),
        P("grp", None),
    )
    return jax.shard_map(
        per_device, mesh=mesh, in_specs=placed, out_specs=P("grp", "ctx"), check_vma=False
    )
```

```python
import functools
import math

import jax
import jax.numpy as jnp
from jax import lax
from jax.experimental import pallas as pl
from jax.experimental.pallas import tpu as pltpu
from jax.sharding import PartitionSpec as P

NOPE = 128
ROPE = 64
PAIR = 2
BLOCK = 64
LANES = 128
F32 = jnp.float32
BF16 = jnp.bfloat16
MESH = pl.DeviceIdType.MESH


def dot(a, b):
    return jnp.dot(a, b, preferred_element_type=F32)


def split3(value):
    high = value.astype(BF16).astype(F32)
    mid = (value - high).astype(BF16).astype(F32)
    return high, mid, value - high - mid


def kernel(
    n, rows, heads, lat, pad,
    lengths, blocks, hidden, q_gain, kv_gain,
    q_down, kv_down, q_up, w_uk, cache, w_uv, o_proj,
    out,
    v_qd, v_kd, v_qu, v_uk, v_ca, v_uv, v_op,
    s1, r1, g2, qf, qs, qall, s4, r4, s5, r5,
    load_sem, pair_sem, send_sem, recv_sem,
):
    me = lax.axis_index("ctx")
    ql = q_down.shape[1]
    kvw = kv_down.shape[1]
    kr = heads * rows
    head_width = NOPE + ROPE
    q_rows = q_up.shape[0]
    o_rows = o_proj.shape[0]
    scale = head_width ** (-0.5)

    loads = []

    def load(src, dst, parts=1):
        mine = []
        size = src.shape[0] // parts
        for part in range(parts):
            where = pl.ds(part * size, size)
            copy = pltpu.make_async_copy(src.at[where], dst.at[where], load_sem.at[len(loads)])
            copy.start()
            loads.append(copy)
            mine.append(copy)
        return mine

    l_qd = load(q_down, v_qd)
    l_kd = load(kv_down, v_kd)
    l_qu = load(q_up, v_qu, 4)
    l_uk = load(w_uk, v_uk)
    core = lax.rem(me, PAIR)
    l_ca = load(cache, v_ca.at[core])
    l_uv = load(w_uv, v_uv)
    l_op = load(o_proj, v_op, 8)

    def arrive(copies):
        for copy in copies:
            copy.wait()

    everyone = (n, me, lambda index: index)
    alike = (n // PAIR, me // PAIR, lambda index: index * PAIR + core)

    def remote(phase, src, dst, device):
        return pltpu.make_async_remote_copy(
            src_ref=src, dst_ref=dst, send_sem=send_sem.at[phase], recv_sem=recv_sem.at[phase],
            device_id={"ctx": device}, device_id_type=MESH,
        )

    def around(mine, k, size):
        peer = mine + k
        return jnp.where(peer >= size, peer - size, peer)

    def for_peers(team, body):
        size, mine, _ = team
        if size <= 16:
            for k in range(1, size):
                body(around(mine, k, size))
        else:
            lax.fori_loop(1, size, lambda k, _: (body(around(mine, k, size)), 0)[1], 0)

    barrier = pltpu.get_barrier_semaphore()
    for_peers(everyone, lambda peer: pl.semaphore_signal(
        barrier, inc=1, device_id={"ctx": peer}, device_id_type=MESH
    ))

    def send_all(phase, team, source, dst):
        _, mine, device = team
        for_peers(
            team, lambda peer: remote(phase, source(peer), dst.at[mine], device(peer)).start()
        )

    def whole(phase, team, dst):
        view = dst.at[pl.ds(0, team[0] - 1)]
        return remote(phase, view, view, around(me, 1, n))

    def wait_all(phase, team, dst):
        whole(phase, team, dst).wait_recv()

    q_chunks = ql // LANES
    kv_chunks = -(-kvw // LANES)
    chunks = q_chunks + kv_chunks
    s1[...] = jnp.zeros_like(s1)
    x = hidden[...]
    arrive(l_qd)
    q_part = dot(x, v_qd[...])
    arrive(l_kd)
    kv_part = dot(x, v_kd[...])
    for c in range(chunks):
        d, s = c % n, c // n
        where = pl.ds(s * rows, rows)
        if c < q_chunks:
            s1[d, where, :] = q_part[:, c * LANES:(c + 1) * LANES]
        else:
            begin = (c - q_chunks) * LANES
            width = min(LANES, kvw - begin)
            s1[d, where, :width] = kv_part[:, begin:begin + width]
    r1[me] = s1[me]
    pl.semaphore_wait(barrier, n - 1)
    send_all(0, everyone, lambda peer: s1.at[peer], r1)
    partner = me + 1 - 2 * core
    share = pltpu.make_async_remote_copy(
        src_ref=cache, dst_ref=v_ca.at[core], send_sem=pair_sem.at[0], recv_sem=pair_sem.at[1],
        device_id={"ctx": partner}, device_id_type=MESH,
    )
    share.start()

    tokens = cache.shape[2]
    token = lax.broadcasted_iota(jnp.int32, (1, PAIR * tokens), 1)
    position = (me - core) * tokens + token
    block_of = position // BLOCK
    used = []
    for r in range(rows):
        hit = block_of == blocks[r, 0]
        for k in range(1, blocks.shape[1]):
            hit = hit | (block_of == blocks[r, k])
        used.append(jnp.where(hit & (position < lengths[r]), 1.0, 0.0))
    used = jnp.concatenate(used, axis=1)
    shape = (n // PAIR * pad, rows * PAIR * tokens)
    row_of_token = lax.broadcasted_iota(jnp.int32, shape, 1) // (PAIR * tokens)
    row_of_query = lax.broadcasted_iota(jnp.int32, shape, 0) % rows
    valid = (row_of_token == row_of_query) & (used > 0.5)
    if pad > kr:
        qs[...] = jnp.zeros_like(qs)

    wait_all(0, everyone, r1)
    g2[me] = jnp.sum(r1[...], axis=0)
    send_all(1, everyone, lambda peer: g2.at[me], g2)
    wait_all(1, everyone, g2)

    def chunk(c):
        return g2[c % n, pl.ds((c // n) * rows, rows), :]

    q_low = jnp.concatenate([chunk(c) for c in range(q_chunks)], axis=1)
    kv_new = jnp.concatenate([chunk(c) for c in range(q_chunks, chunks)], axis=1)[:, :kvw]
    q_mean = jnp.sum(q_low * q_low, axis=1, keepdims=True) * (1.0 / ql)
    gain = jnp.concatenate([q_gain[c:c + 1, :] for c in range(q_chunks)], axis=1)
    q_normed = (q_low * lax.rsqrt(q_mean + 1e-06) * gain).astype(BF16)
    arrive(l_qu)
    qf[...] = dot(q_normed, v_qu[...]).astype(BF16).astype(F32)
    arrive(l_uk)
    for h in range(heads):
        nope = qf[:, h * head_width:h * head_width + NOPE].astype(BF16)
        where = pl.ds(h * rows, rows)
        qs[where, :lat] = dot(nope, v_uk[h])
        qs[where, lat:] = qf[:, h * head_width + NOPE:(h + 1) * head_width]
    query = qs[...].astype(BF16)
    qall[me // PAIR] = query
    send_all(2, alike, lambda peer: qall.at[me // PAIR], qall)

    kv_lat = kv_new[:, :lat]
    kv_mean = jnp.sum(kv_lat * kv_lat, axis=1, keepdims=True) * (1.0 / lat)
    lat_new = kv_lat * lax.rsqrt(kv_mean + 1e-06) * kv_gain[...]
    key_new = jnp.concatenate([lat_new, kv_new[:, lat:]], axis=1).astype(BF16).astype(F32)
    own_row = lax.broadcasted_iota(jnp.int32, (pad, kvw), 0) % rows
    key_rows = jnp.broadcast_to(key_new[0:1], (pad, kvw))
    for r in range(1, rows):
        key_rows = jnp.where(own_row == r, jnp.broadcast_to(key_new[r:r + 1], (pad, kvw)), key_rows)
    own = scale * jnp.sum(query.astype(F32) * key_rows, axis=1, keepdims=True)

    arrive(l_ca)
    pltpu.make_async_remote_copy(
        src_ref=cache, dst_ref=v_ca.at[1 - core], send_sem=pair_sem.at[0], recv_sem=pair_sem.at[1],
        device_id={"ctx": partner}, device_id_type=MESH,
    ).wait()
    wait_all(2, alike, qall)
    q_mat = qall[...].reshape(n // PAIR * pad, kvw)
    parts = [(half, r) for r in range(rows) for half in range(PAIR)]
    score = scale * jnp.concatenate([dot(q_mat, v_ca[half, r]) for half, r in parts], axis=1)
    peak = jnp.max(jnp.where(valid, score, -1e30), axis=1, keepdims=True)
    expo = jnp.where(valid, jnp.exp(score - peak), 0.0)
    total = jnp.sum(expo, axis=1, keepdims=True)
    weights = expo.astype(BF16)
    numer = jnp.zeros((n // PAIR * pad, lat), F32)
    for place, (half, r) in enumerate(parts):
        numer = numer + lax.dot_general(
            weights[:, place * tokens:(place + 1) * tokens], v_ca[half, r, :lat, :],
            (((1,), (1,)), ((), ())), preferred_element_type=F32,
        )
    s4[:, :, :lat] = numer.astype(BF16).reshape(n // PAIR, pad, lat)
    lane = lax.broadcasted_iota(jnp.int32, (n // PAIR * pad, LANES), 1)
    stats = jnp.zeros((n // PAIR * pad, LANES), F32)
    for place, piece in enumerate(split3(peak) + split3(total)):
        stats = jnp.where(lane == place, piece, stats)
    s4[:, :, lat:] = stats.astype(BF16).reshape(n // PAIR, pad, LANES)
    send_all(3, alike, lambda peer: s4.at[peer], r4)
    r4[me // PAIR] = s4[me // PAIR]
    wait_all(3, alike, r4)

    got = r4[:, :, lat:].astype(F32)
    peaks = got[:, :, 0:1] + got[:, :, 1:2] + got[:, :, 2:3]
    totals = got[:, :, 3:4] + got[:, :, 4:5] + got[:, :, 5:6]
    top = jnp.maximum(jnp.max(peaks, axis=0), own)
    factor = jnp.exp(peaks - top[None])
    own_weight = jnp.exp(own - top)
    denom = jnp.sum(totals * factor, axis=0) + own_weight
    mixed = own_weight * key_rows[:, :lat]
    for d in range(n // PAIR):
        mixed = mixed + factor[d] * r4[d, :, :lat].astype(F32)
    latent = (mixed / denom).astype(BF16).astype(F32)
    arrive(l_uv)
    head_out = jnp.concatenate(
        [dot(latent[h * rows:(h + 1) * rows].astype(BF16), v_uv[h]) for h in range(heads)], axis=1
    ).astype(BF16)

    arrive(l_op)
    width = out.shape[1]
    group = math.lcm(width, 2 * LANES)
    for g in range(n * width // group):
        part = dot(head_out, v_op[:, g * group:(g + 1) * group])
        for i in range(group // width):
            d = g * (group // width) + i
            s5[d] = part[:, i * width:(i + 1) * width]

            @pl.when(me != d)
            def _():
                remote(4, s5.at[d], r5.at[me], d).start()

    r5[me] = s5[me]
    wait_all(4, everyone, r5)
    out[...] = jnp.sum(r5[...], axis=0).astype(BF16)
    for phase, team, dst in (
        (0, everyone, r1), (1, everyone, g2), (2, alike, qall), (3, alike, r4), (4, everyone, r5)
    ):
        whole(phase, team, dst).wait_send()


def solution(mesh):
    n = mesh.shape["ctx"]

    def per_device(
        hidden, q_down, q_gain, q_up, w_uk, kv_down, kv_gain, w_uv, o_proj, cache, lengths, blocks
    ):
        rows = hidden.shape[0]
        heads, _, lat = w_uk.shape
        kvw = kv_down.shape[1]
        width = o_proj.shape[1] // n
        pad = -(-rows * heads // 16) * 16
        chunks = q_down.shape[1] // LANES + -(-kvw // LANES)
        held = -(-chunks // n) * rows
        vmem = pl.BlockSpec(memory_space=pltpu.VMEM)
        smem = pl.BlockSpec(memory_space=pltpu.SMEM)
        hbm = pl.BlockSpec(memory_space=pl.ANY)
        cache = jnp.swapaxes(cache, 1, 2)
        big = (q_down, kv_down, q_up, w_uk, cache, w_uv, o_proj)
        held_in = [a.shape for a in big]
        held_in[4] = (PAIR,) + cache.shape
        return pl.pallas_call(
            functools.partial(kernel, n, rows, heads, lat, pad),
            out_shape=jax.ShapeDtypeStruct((rows, width), BF16),
            in_specs=[smem, smem, vmem, vmem, vmem] + [hbm] * len(big),
            out_specs=vmem,
            scratch_shapes=[pltpu.VMEM(shape, BF16) for shape in held_in] + [
                pltpu.VMEM((n, held, LANES), F32),
                pltpu.VMEM((n, held, LANES), F32),
                pltpu.VMEM((n, held, LANES), F32),
                pltpu.VMEM((rows, q_up.shape[1]), F32),
                pltpu.VMEM((pad, kvw), F32),
                pltpu.VMEM((n // PAIR, pad, kvw), BF16),
                pltpu.VMEM((n // PAIR, pad, lat + LANES), BF16),
                pltpu.VMEM((n // PAIR, pad, lat + LANES), BF16),
                pltpu.VMEM((n, rows, width), F32),
                pltpu.VMEM((n, rows, width), F32),
                pltpu.SemaphoreType.DMA((17,)),
                pltpu.SemaphoreType.DMA((2,)),
                pltpu.SemaphoreType.DMA((5,)),
                pltpu.SemaphoreType.DMA((5,)),
            ],
            compiler_params=pltpu.CompilerParams(
                collective_id=0, has_side_effects=True, vmem_limit_bytes=56 * 1024 * 1024
            ),
        )(lengths, blocks, hidden, q_gain.reshape(-1, LANES), kv_gain[None], *big)

    placed = (
        P("grp", "ctx"),
        P("ctx", None),
        P(),
        P(None, "ctx"),
        P("ctx", None, None),
        P("ctx", None),
        P(),
        P("ctx", None, None),
        P("ctx", None),
        P("grp", "ctx", None),
        P("grp"),
        P("grp", None),
    )
    return jax.shard_map(
        per_device, mesh=mesh, in_specs=placed, out_specs=P("grp", "ctx"), check_vma=False
    )
```

```python
import functools
import math

import jax
import jax.numpy as jnp
from jax import lax
from jax.experimental import pallas as pl
from jax.experimental.pallas import tpu as pltpu
from jax.sharding import PartitionSpec as P

NOPE = 128
ROPE = 64
PAIR = 2
BLOCK = 64
LANES = 128
F32 = jnp.float32
BF16 = jnp.bfloat16
MESH = pl.DeviceIdType.MESH


def dot(a, b):
    return jnp.dot(a, b, preferred_element_type=F32)


def split3(value):
    high = value.astype(BF16).astype(F32)
    mid = (value - high).astype(BF16).astype(F32)
    return high, mid, value - high - mid


def kernel(
    n, rows, heads, lat, pad,
    lengths, blocks, hidden, q_gain, kv_gain,
    q_down, kv_down, q_up, w_uk, cache, w_uv, o_proj,
    out,
    v_qd, v_kd, v_qu, v_uk, v_ca, v_uv, v_op, v_ct,
    s1, r1, g2, qf, qs, qall, s4, r4, s5, r5,
    load_sem, pair_sem, send_sem, recv_sem,
):
    me = lax.axis_index("ctx")
    ql = q_down.shape[1]
    kvw = kv_down.shape[1]
    kr = heads * rows
    head_width = NOPE + ROPE
    q_rows = q_up.shape[0]
    o_rows = o_proj.shape[0]
    scale = head_width ** (-0.5)

    loads = []

    def load(src, dst, parts=1):
        mine = []
        size = src.shape[0] // parts
        for part in range(parts):
            where = pl.ds(part * size, size)
            copy = pltpu.make_async_copy(src.at[where], dst.at[where], load_sem.at[len(loads)])
            copy.start()
            loads.append(copy)
            mine.append(copy)
        return mine

    l_qd = load(q_down, v_qd)
    l_kd = load(kv_down, v_kd)
    l_qu = load(q_up, v_qu, 4)
    l_uk = load(w_uk, v_uk)
    core = lax.rem(me, PAIR)
    l_ca = load(cache, v_ca.at[core])
    l_uv = load(w_uv, v_uv)
    l_op = load(o_proj, v_op, 8)

    def arrive(copies):
        for copy in copies:
            copy.wait()

    everyone = (n, me, lambda index: index)
    alike = (n // PAIR, me // PAIR, lambda index: index * PAIR + core)

    def remote(phase, src, dst, device):
        return pltpu.make_async_remote_copy(
            src_ref=src, dst_ref=dst, send_sem=send_sem.at[phase], recv_sem=recv_sem.at[phase],
            device_id={"ctx": device}, device_id_type=MESH,
        )

    def around(mine, k, size):
        peer = mine + k
        return jnp.where(peer >= size, peer - size, peer)

    def for_peers(team, body):
        size, mine, _ = team
        if size <= 16:
            for k in range(1, size):
                body(around(mine, k, size))
        else:
            lax.fori_loop(1, size, lambda k, _: (body(around(mine, k, size)), 0)[1], 0)

    barrier = pltpu.get_barrier_semaphore()
    for_peers(everyone, lambda peer: pl.semaphore_signal(
        barrier, inc=1, device_id={"ctx": peer}, device_id_type=MESH
    ))

    def send_all(phase, team, source, dst):
        _, mine, device = team
        for_peers(
            team, lambda peer: remote(phase, source(peer), dst.at[mine], device(peer)).start()
        )

    def whole(phase, team, dst):
        view = dst.at[pl.ds(0, team[0] - 1)]
        return remote(phase, view, view, around(me, 1, n))

    def wait_all(phase, team, dst):
        whole(phase, team, dst).wait_recv()

    q_chunks = ql // LANES
    kv_chunks = -(-kvw // LANES)
    chunks = q_chunks + kv_chunks
    s1[...] = jnp.zeros_like(s1)
    x = hidden[...]
    arrive(l_qd)
    q_part = dot(x, v_qd[...])
    arrive(l_kd)
    kv_part = dot(x, v_kd[...])
    for c in range(chunks):
        d, s = c % n, c // n
        where = pl.ds(s * rows, rows)
        if c < q_chunks:
            s1[d, where, :] = q_part[:, c * LANES:(c + 1) * LANES]
        else:
            begin = (c - q_chunks) * LANES
            width = min(LANES, kvw - begin)
            s1[d, where, :width] = kv_part[:, begin:begin + width]
    r1[me] = s1[me]
    pl.semaphore_wait(barrier, n - 1)
    send_all(0, everyone, lambda peer: s1.at[peer], r1)
    partner = me + 1 - 2 * core
    share = pltpu.make_async_remote_copy(
        src_ref=cache, dst_ref=v_ca.at[core], send_sem=pair_sem.at[0], recv_sem=pair_sem.at[1],
        device_id={"ctx": partner}, device_id_type=MESH,
    )
    share.start()

    tokens = cache.shape[2]
    token = lax.broadcasted_iota(jnp.int32, (1, PAIR * tokens), 1)
    position = (me - core) * tokens + token
    block_of = position // BLOCK
    used = []
    for r in range(rows):
        hit = block_of == blocks[r, 0]
        for k in range(1, blocks.shape[1]):
            hit = hit | (block_of == blocks[r, k])
        used.append(jnp.where(hit & (position < lengths[r]), 1.0, 0.0))
    used = jnp.concatenate(used, axis=1)
    size = n // PAIR
    mine = me // PAIR
    cut = (size + 1) // 2
    shape = (cut * pad, rows * PAIR * tokens)
    row_of_token = lax.broadcasted_iota(jnp.int32, shape, 1) // (PAIR * tokens)
    row_of_query = lax.broadcasted_iota(jnp.int32, shape, 0) % rows
    valid = (row_of_token == row_of_query) & (used > 0.5)
    if pad > kr:
        qs[...] = jnp.zeros_like(qs)

    wait_all(0, everyone, r1)
    g2[me] = jnp.sum(r1[...], axis=0)
    send_all(1, everyone, lambda peer: g2.at[me], g2)
    wait_all(1, everyone, g2)

    def chunk(c):
        return g2[c % n, pl.ds((c // n) * rows, rows), :]

    q_low = jnp.concatenate([chunk(c) for c in range(q_chunks)], axis=1)
    kv_new = jnp.concatenate([chunk(c) for c in range(q_chunks, chunks)], axis=1)[:, :kvw]
    q_mean = jnp.sum(q_low * q_low, axis=1, keepdims=True) * (1.0 / ql)
    gain = jnp.concatenate([q_gain[c:c + 1, :] for c in range(q_chunks)], axis=1)
    q_normed = (q_low * lax.rsqrt(q_mean + 1e-06) * gain).astype(BF16)
    arrive(l_qu)
    qf[...] = dot(q_normed, v_qu[...]).astype(BF16).astype(F32)
    arrive(l_uk)
    for h in range(heads):
        nope = qf[:, h * head_width:h * head_width + NOPE].astype(BF16)
        where = pl.ds(h * rows, rows)
        qs[where, :lat] = dot(nope, v_uk[h])
        qs[where, lat:] = qf[:, h * head_width + NOPE:(h + 1) * head_width]
    query = qs[...].astype(BF16)
    qall[0] = query
    for k in range(1, size):
        device = alike[2](around(mine, k, size))
        remote(2 if k < cut else 3, qall.at[0], qall.at[k], device).start()

    kv_lat = kv_new[:, :lat]
    kv_mean = jnp.sum(kv_lat * kv_lat, axis=1, keepdims=True) * (1.0 / lat)
    lat_new = kv_lat * lax.rsqrt(kv_mean + 1e-06) * kv_gain[...]
    key_new = jnp.concatenate([lat_new, kv_new[:, lat:]], axis=1).astype(BF16).astype(F32)
    own_row = lax.broadcasted_iota(jnp.int32, (pad, kvw), 0) % rows
    key_rows = jnp.broadcast_to(key_new[0:1], (pad, kvw))
    for r in range(1, rows):
        key_rows = jnp.where(own_row == r, jnp.broadcast_to(key_new[r:r + 1], (pad, kvw)), key_rows)
    own = scale * jnp.sum(query.astype(F32) * key_rows, axis=1, keepdims=True)

    arrive(l_ca)
    pltpu.make_async_remote_copy(
        src_ref=cache, dst_ref=v_ca.at[1 - core], send_sem=pair_sem.at[0], recv_sem=pair_sem.at[1],
        device_id={"ctx": partner}, device_id_type=MESH,
    ).wait()
    parts = [(half, r) for r in range(rows) for half in range(PAIR)]
    for place, (half, r) in enumerate(parts):
        v_ct[place * tokens:(place + 1) * tokens, :] = v_ca[half, r, :lat, :].T

    def arrived(phase, ref, begin, count):
        view = ref.at[pl.ds(begin, count)]
        return remote(phase, view, view, around(me, 1, n))

    stages = [(2, 0, cut), (3, cut, size - cut)]
    for phase, begin, count in stages:
        skip = 1 if begin == 0 else 0
        arrived(phase, qall, begin + skip, count - skip).wait_recv()
        q_mat = qall[begin:begin + count].reshape(count * pad, kvw)
        score = scale * jnp.concatenate([dot(q_mat, v_ca[half, r]) for half, r in parts], axis=1)
        here = valid[:count * pad]
        peak = jnp.max(jnp.where(here, score, -1e30), axis=1, keepdims=True)
        expo = jnp.where(here, jnp.exp(score - peak), 0.0)
        total = jnp.sum(expo, axis=1, keepdims=True)
        numer = dot(expo.astype(BF16), v_ct[...])
        s4[begin:begin + count, :, :lat] = numer.astype(BF16).reshape(count, pad, lat)
        lane = lax.broadcasted_iota(jnp.int32, (count * pad, LANES), 1)
        stats = jnp.zeros((count * pad, LANES), F32)
        for place, piece in enumerate(split3(peak) + split3(total)):
            stats = jnp.where(lane == place, piece, stats)
        s4[begin:begin + count, :, lat:] = stats.astype(BF16).reshape(count, pad, LANES)
        for k in range(begin + skip, begin + count):
            device = alike[2](around(mine, size - k, size))
            remote(4, s4.at[k], r4.at[k], device).start()
    r4[0] = s4[0]
    wait_all(4, alike, r4)

    got = r4[:, :, lat:].astype(F32)
    peaks = got[:, :, 0:1] + got[:, :, 1:2] + got[:, :, 2:3]
    totals = got[:, :, 3:4] + got[:, :, 4:5] + got[:, :, 5:6]
    top = jnp.maximum(jnp.max(peaks, axis=0), own)
    factor = jnp.exp(peaks - top[None])
    own_weight = jnp.exp(own - top)
    denom = jnp.sum(totals * factor, axis=0) + own_weight
    mixed = own_weight * key_rows[:, :lat]
    for d in range(n // PAIR):
        mixed = mixed + factor[d] * r4[d, :, :lat].astype(F32)
    latent = (mixed / denom).astype(BF16).astype(F32)
    arrive(l_uv)
    head_out = jnp.concatenate(
        [dot(latent[h * rows:(h + 1) * rows].astype(BF16), v_uv[h]) for h in range(heads)], axis=1
    ).astype(BF16)

    arrive(l_op)
    width = out.shape[1]
    group = math.lcm(width, 2 * LANES)
    for g in range(n * width // group):
        part = dot(head_out, v_op[:, g * group:(g + 1) * group])
        for i in range(group // width):
            d = g * (group // width) + i
            s5[d] = part[:, i * width:(i + 1) * width]

            @pl.when(me != d)
            def _():
                remote(5, s5.at[d], r5.at[me], d).start()

    r5[me] = s5[me]
    wait_all(5, everyone, r5)
    out[...] = jnp.sum(r5[...], axis=0).astype(BF16)
    for phase, team, dst in (
        (0, everyone, r1), (1, everyone, g2), (4, alike, r4), (5, everyone, r5)
    ):
        whole(phase, team, dst).wait_send()
    for phase, begin, count in stages:
        skip = 1 if begin == 0 else 0
        arrived(phase, qall, begin + skip, count - skip).wait_send()


def solution(mesh):
    n = mesh.shape["ctx"]

    def per_device(
        hidden, q_down, q_gain, q_up, w_uk, kv_down, kv_gain, w_uv, o_proj, cache, lengths, blocks
    ):
        rows = hidden.shape[0]
        heads, _, lat = w_uk.shape
        kvw = kv_down.shape[1]
        width = o_proj.shape[1] // n
        pad = -(-rows * heads // 16) * 16
        chunks = q_down.shape[1] // LANES + -(-kvw // LANES)
        held = -(-chunks // n) * rows
        vmem = pl.BlockSpec(memory_space=pltpu.VMEM)
        smem = pl.BlockSpec(memory_space=pltpu.SMEM)
        hbm = pl.BlockSpec(memory_space=pl.ANY)
        cache = jnp.swapaxes(cache, 1, 2)
        big = (q_down, kv_down, q_up, w_uk, cache, w_uv, o_proj)
        held_in = [a.shape for a in big]
        held_in[4] = (PAIR,) + cache.shape
        return pl.pallas_call(
            functools.partial(kernel, n, rows, heads, lat, pad),
            out_shape=jax.ShapeDtypeStruct((rows, width), BF16),
            in_specs=[smem, smem, vmem, vmem, vmem] + [hbm] * len(big),
            out_specs=vmem,
            scratch_shapes=[pltpu.VMEM(shape, BF16) for shape in held_in] + [
                pltpu.VMEM((PAIR * rows * cache.shape[2], lat), BF16),
                pltpu.VMEM((n, held, LANES), F32),
                pltpu.VMEM((n, held, LANES), F32),
                pltpu.VMEM((n, held, LANES), F32),
                pltpu.VMEM((rows, q_up.shape[1]), F32),
                pltpu.VMEM((pad, kvw), F32),
                pltpu.VMEM((n // PAIR, pad, kvw), BF16),
                pltpu.VMEM((n // PAIR, pad, lat + LANES), BF16),
                pltpu.VMEM((n // PAIR, pad, lat + LANES), BF16),
                pltpu.VMEM((n, rows, width), F32),
                pltpu.VMEM((n, rows, width), F32),
                pltpu.SemaphoreType.DMA((17,)),
                pltpu.SemaphoreType.DMA((2,)),
                pltpu.SemaphoreType.DMA((6,)),
                pltpu.SemaphoreType.DMA((6,)),
            ],
            compiler_params=pltpu.CompilerParams(
                collective_id=0, has_side_effects=True, vmem_limit_bytes=56 * 1024 * 1024
            ),
        )(lengths, blocks, hidden, q_gain.reshape(-1, LANES), kv_gain[None], *big)

    placed = (
        P("grp", "ctx"),
        P("ctx", None),
        P(),
        P(None, "ctx"),
        P("ctx", None, None),
        P("ctx", None),
        P(),
        P("ctx", None, None),
        P("ctx", None),
        P("grp", "ctx", None),
        P("grp"),
        P("grp", None),
    )
    return jax.shard_map(
        per_device, mesh=mesh, in_specs=placed, out_specs=P("grp", "ctx"), check_vma=False
    )
```

```python
import functools
import math

import jax
import jax.numpy as jnp
from jax import lax
from jax.experimental import pallas as pl
from jax.experimental.pallas import tpu as pltpu
from jax.sharding import PartitionSpec as P

NOPE = 128
ROPE = 64
PAIR = 2
BLOCK = 64
LANES = 128
F32 = jnp.float32
BF16 = jnp.bfloat16
MESH = pl.DeviceIdType.MESH


def dot(a, b):
    return jnp.dot(a, b, preferred_element_type=F32)


def split3(value):
    high = value.astype(BF16).astype(F32)
    mid = (value - high).astype(BF16).astype(F32)
    return high, mid, value - high - mid


def kernel(
    n, rows, heads, lat, pad,
    lengths, blocks, hidden, q_gain, kv_gain,
    q_down, kv_down, q_up, w_uk, cache, w_uv, o_proj,
    out,
    v_qd, v_kd, v_qu, v_uk, v_ca, v_uv, v_op, v_ct,
    s1, r1, g2, qf, qs, qall, s4, r4, s5, r5,
    load_sem, pair_sem, send_sem, recv_sem,
):
    me = lax.axis_index("ctx")
    ql = q_down.shape[1]
    kvw = kv_down.shape[1]
    kr = heads * rows
    head_width = NOPE + ROPE
    q_rows = q_up.shape[0]
    o_rows = o_proj.shape[0]
    scale = head_width ** (-0.5)

    loads = []

    def load(src, dst, parts=1):
        mine = []
        size = src.shape[0] // parts
        for part in range(parts):
            where = pl.ds(part * size, size)
            copy = pltpu.make_async_copy(src.at[where], dst.at[where], load_sem.at[len(loads)])
            copy.start()
            loads.append(copy)
            mine.append(copy)
        return mine

    l_qd = load(q_down, v_qd)
    l_kd = load(kv_down, v_kd)
    core = lax.rem(me, PAIR)

    def arrive(copies):
        for copy in copies:
            copy.wait()

    everyone = (n, me, lambda index: index)
    alike = (n // PAIR, me // PAIR, lambda index: index * PAIR + core)

    def remote(phase, src, dst, device):
        return pltpu.make_async_remote_copy(
            src_ref=src, dst_ref=dst, send_sem=send_sem.at[phase], recv_sem=recv_sem.at[phase],
            device_id={"ctx": device}, device_id_type=MESH,
        )

    def around(mine, k, size):
        peer = mine + k
        return jnp.where(peer >= size, peer - size, peer)

    def for_peers(team, body):
        size, mine, _ = team
        if size <= 16:
            for k in range(1, size):
                body(around(mine, k, size))
        else:
            lax.fori_loop(1, size, lambda k, _: (body(around(mine, k, size)), 0)[1], 0)

    barrier = pltpu.get_barrier_semaphore()
    for_peers(everyone, lambda peer: pl.semaphore_signal(
        barrier, inc=1, device_id={"ctx": peer}, device_id_type=MESH
    ))

    def send_all(phase, team, source, dst):
        _, mine, device = team
        for_peers(
            team, lambda peer: remote(phase, source(peer), dst.at[mine], device(peer)).start()
        )

    def whole(phase, team, dst):
        view = dst.at[pl.ds(0, team[0] - 1)]
        return remote(phase, view, view, around(me, 1, n))

    def wait_all(phase, team, dst):
        whole(phase, team, dst).wait_recv()

    q_chunks = ql // LANES
    kv_chunks = -(-kvw // LANES)
    chunks = q_chunks + kv_chunks
    s1[...] = jnp.zeros_like(s1)
    x = hidden[...]
    arrive(l_qd)
    q_part = dot(x, v_qd[...])
    arrive(l_kd)
    kv_part = dot(x, v_kd[...])
    for c in range(chunks):
        d, s = c % n, c // n
        where = pl.ds(s * rows, rows)
        if c < q_chunks:
            s1[d, where, :] = q_part[:, c * LANES:(c + 1) * LANES]
        else:
            begin = (c - q_chunks) * LANES
            width = min(LANES, kvw - begin)
            s1[d, where, :width] = kv_part[:, begin:begin + width]
    r1[me] = s1[me]
    pl.semaphore_wait(barrier, n - 1)
    send_all(0, everyone, lambda peer: s1.at[peer], r1)
    l_qu = load(q_up, v_qu, 4)
    l_uk = load(w_uk, v_uk)
    l_ca = load(cache, v_ca.at[core])

    tokens = cache.shape[2]
    token = lax.broadcasted_iota(jnp.int32, (1, PAIR * tokens), 1)
    position = (me - core) * tokens + token
    block_of = position // BLOCK
    used = []
    for r in range(rows):
        hit = block_of == blocks[r, 0]
        for k in range(1, blocks.shape[1]):
            hit = hit | (block_of == blocks[r, k])
        used.append(jnp.where(hit & (position < lengths[r]), 1.0, 0.0))
    used = jnp.concatenate(used, axis=1)
    size = n // PAIR
    mine = me // PAIR
    cut = (size + 1) // 2
    shape = (cut * pad, rows * PAIR * tokens)
    row_of_token = lax.broadcasted_iota(jnp.int32, shape, 1) // (PAIR * tokens)
    row_of_query = lax.broadcasted_iota(jnp.int32, shape, 0) % rows
    valid = (row_of_token == row_of_query) & (used > 0.5)
    if pad > kr:
        qs[...] = jnp.zeros_like(qs)

    wait_all(0, everyone, r1)
    g2[me] = jnp.sum(r1[...], axis=0)
    send_all(1, everyone, lambda peer: g2.at[me], g2)
    partner = me + 1 - 2 * core
    share = pltpu.make_async_remote_copy(
        src_ref=cache, dst_ref=v_ca.at[core], send_sem=pair_sem.at[0], recv_sem=pair_sem.at[1],
        device_id={"ctx": partner}, device_id_type=MESH,
    )
    share.start()
    l_uv = load(w_uv, v_uv)
    l_op = load(o_proj, v_op, 8)
    wait_all(1, everyone, g2)

    def chunk(c):
        return g2[c % n, pl.ds((c // n) * rows, rows), :]

    q_low = jnp.concatenate([chunk(c) for c in range(q_chunks)], axis=1)
    kv_new = jnp.concatenate([chunk(c) for c in range(q_chunks, chunks)], axis=1)[:, :kvw]
    q_mean = jnp.sum(q_low * q_low, axis=1, keepdims=True) * (1.0 / ql)
    gain = jnp.concatenate([q_gain[c:c + 1, :] for c in range(q_chunks)], axis=1)
    q_normed = (q_low * lax.rsqrt(q_mean + 1e-06) * gain).astype(BF16)
    arrive(l_qu)
    qf[...] = dot(q_normed, v_qu[...]).astype(BF16).astype(F32)
    arrive(l_uk)
    for h in range(heads):
        nope = qf[:, h * head_width:h * head_width + NOPE].astype(BF16)
        where = pl.ds(h * rows, rows)
        qs[where, :lat] = dot(nope, v_uk[h])
        qs[where, lat:] = qf[:, h * head_width + NOPE:(h + 1) * head_width]
    query = qs[...].astype(BF16)
    qall[0] = query
    for k in range(1, size):
        device = alike[2](around(mine, k, size))
        remote(2 if k < cut else 3, qall.at[0], qall.at[k], device).start()

    kv_lat = kv_new[:, :lat]
    kv_mean = jnp.sum(kv_lat * kv_lat, axis=1, keepdims=True) * (1.0 / lat)
    lat_new = kv_lat * lax.rsqrt(kv_mean + 1e-06) * kv_gain[...]
    key_new = jnp.concatenate([lat_new, kv_new[:, lat:]], axis=1).astype(BF16).astype(F32)
    own_row = lax.broadcasted_iota(jnp.int32, (pad, kvw), 0) % rows
    key_rows = jnp.broadcast_to(key_new[0:1], (pad, kvw))
    for r in range(1, rows):
        key_rows = jnp.where(own_row == r, jnp.broadcast_to(key_new[r:r + 1], (pad, kvw)), key_rows)
    own = scale * jnp.sum(query.astype(F32) * key_rows, axis=1, keepdims=True)

    arrive(l_ca)
    pltpu.make_async_remote_copy(
        src_ref=cache, dst_ref=v_ca.at[1 - core], send_sem=pair_sem.at[0], recv_sem=pair_sem.at[1],
        device_id={"ctx": partner}, device_id_type=MESH,
    ).wait()
    parts = [(half, r) for r in range(rows) for half in range(PAIR)]
    for place, (half, r) in enumerate(parts):
        v_ct[place * tokens:(place + 1) * tokens, :] = v_ca[half, r, :lat, :].T

    def arrived(phase, ref, begin, count):
        view = ref.at[pl.ds(begin, count)]
        return remote(phase, view, view, around(me, 1, n))

    stages = [(2, 0, cut), (3, cut, size - cut)]
    for phase, begin, count in stages:
        skip = 1 if begin == 0 else 0
        arrived(phase, qall, begin + skip, count - skip).wait_recv()
        q_mat = qall[begin:begin + count].reshape(count * pad, kvw)
        score = scale * jnp.concatenate([dot(q_mat, v_ca[half, r]) for half, r in parts], axis=1)
        here = valid[:count * pad]
        peak = jnp.max(jnp.where(here, score, -1e30), axis=1, keepdims=True)
        expo = jnp.where(here, jnp.exp(score - peak), 0.0)
        total = jnp.sum(expo, axis=1, keepdims=True)
        numer = dot(expo.astype(BF16), v_ct[...])
        s4[begin:begin + count, :, :lat] = numer.astype(BF16).reshape(count, pad, lat)
        lane = lax.broadcasted_iota(jnp.int32, (count * pad, LANES), 1)
        stats = jnp.zeros((count * pad, LANES), F32)
        for place, piece in enumerate(split3(peak) + split3(total)):
            stats = jnp.where(lane == place, piece, stats)
        s4[begin:begin + count, :, lat:] = stats.astype(BF16).reshape(count, pad, LANES)
        for k in range(begin + skip, begin + count):
            device = alike[2](around(mine, size - k, size))
            remote(4, s4.at[k], r4.at[k], device).start()
    r4[0] = s4[0]
    wait_all(4, alike, r4)

    got = r4[:, :, lat:].astype(F32)
    peaks = got[:, :, 0:1] + got[:, :, 1:2] + got[:, :, 2:3]
    totals = got[:, :, 3:4] + got[:, :, 4:5] + got[:, :, 5:6]
    top = jnp.maximum(jnp.max(peaks, axis=0), own)
    factor = jnp.exp(peaks - top[None])
    own_weight = jnp.exp(own - top)
    denom = jnp.sum(totals * factor, axis=0) + own_weight
    mixed = own_weight * key_rows[:, :lat]
    for d in range(n // PAIR):
        mixed = mixed + factor[d] * r4[d, :, :lat].astype(F32)
    latent = (mixed / denom).astype(BF16).astype(F32)
    arrive(l_uv)
    head_out = jnp.concatenate(
        [dot(latent[h * rows:(h + 1) * rows].astype(BF16), v_uv[h]) for h in range(heads)], axis=1
    ).astype(BF16)

    arrive(l_op)
    width = out.shape[1]
    group = math.lcm(width, 2 * LANES)
    for g in range(n * width // group):
        part = dot(head_out, v_op[:, g * group:(g + 1) * group])
        for i in range(group // width):
            d = g * (group // width) + i
            s5[d] = part[:, i * width:(i + 1) * width]

            @pl.when(me != d)
            def _():
                remote(5, s5.at[d], r5.at[me], d).start()

    r5[me] = s5[me]
    wait_all(5, everyone, r5)
    out[...] = jnp.sum(r5[...], axis=0).astype(BF16)
    for phase, team, dst in (
        (0, everyone, r1), (1, everyone, g2), (4, alike, r4), (5, everyone, r5)
    ):
        whole(phase, team, dst).wait_send()
    for phase, begin, count in stages:
        skip = 1 if begin == 0 else 0
        arrived(phase, qall, begin + skip, count - skip).wait_send()


def solution(mesh):
    n = mesh.shape["ctx"]

    def per_device(
        hidden, q_down, q_gain, q_up, w_uk, kv_down, kv_gain, w_uv, o_proj, cache, lengths, blocks
    ):
        rows = hidden.shape[0]
        heads, _, lat = w_uk.shape
        kvw = kv_down.shape[1]
        width = o_proj.shape[1] // n
        pad = -(-rows * heads // 16) * 16
        chunks = q_down.shape[1] // LANES + -(-kvw // LANES)
        held = -(-chunks // n) * rows
        vmem = pl.BlockSpec(memory_space=pltpu.VMEM)
        smem = pl.BlockSpec(memory_space=pltpu.SMEM)
        hbm = pl.BlockSpec(memory_space=pl.ANY)
        cache = jnp.swapaxes(cache, 1, 2)
        big = (q_down, kv_down, q_up, w_uk, cache, w_uv, o_proj)
        held_in = [a.shape for a in big]
        held_in[4] = (PAIR,) + cache.shape
        return pl.pallas_call(
            functools.partial(kernel, n, rows, heads, lat, pad),
            out_shape=jax.ShapeDtypeStruct((rows, width), BF16),
            in_specs=[smem, smem, vmem, vmem, vmem] + [hbm] * len(big),
            out_specs=vmem,
            scratch_shapes=[pltpu.VMEM(shape, BF16) for shape in held_in] + [
                pltpu.VMEM((PAIR * rows * cache.shape[2], lat), BF16),
                pltpu.VMEM((n, held, LANES), F32),
                pltpu.VMEM((n, held, LANES), F32),
                pltpu.VMEM((n, held, LANES), F32),
                pltpu.VMEM((rows, q_up.shape[1]), F32),
                pltpu.VMEM((pad, kvw), F32),
                pltpu.VMEM((n // PAIR, pad, kvw), BF16),
                pltpu.VMEM((n // PAIR, pad, lat + LANES), BF16),
                pltpu.VMEM((n // PAIR, pad, lat + LANES), BF16),
                pltpu.VMEM((n, rows, width), F32),
                pltpu.VMEM((n, rows, width), F32),
                pltpu.SemaphoreType.DMA((17,)),
                pltpu.SemaphoreType.DMA((2,)),
                pltpu.SemaphoreType.DMA((6,)),
                pltpu.SemaphoreType.DMA((6,)),
            ],
            compiler_params=pltpu.CompilerParams(
                collective_id=0, has_side_effects=True, vmem_limit_bytes=56 * 1024 * 1024
            ),
        )(lengths, blocks, hidden, q_gain.reshape(-1, LANES), kv_gain[None], *big)

    placed = (
        P("grp", "ctx"),
        P("ctx", None),
        P(),
        P(None, "ctx"),
        P("ctx", None, None),
        P("ctx", None),
        P(),
        P("ctx", None, None),
        P("ctx", None),
        P("grp", "ctx", None),
        P("grp"),
        P("grp", None),
    )
    return jax.shard_map(
        per_device, mesh=mesh, in_specs=placed, out_specs=P("grp", "ctx"), check_vma=False
    )
```

```python
import functools
import math

import jax
import jax.numpy as jnp
from jax import lax
from jax.experimental import pallas as pl
from jax.experimental.pallas import tpu as pltpu
from jax.sharding import PartitionSpec as P

NOPE = 128
ROPE = 64
SHARE = 4
BLOCK = 64
LANES = 128
F32 = jnp.float32
BF16 = jnp.bfloat16
MESH = pl.DeviceIdType.MESH


def dot(a, b):
    return jnp.dot(a, b, preferred_element_type=F32)


def split3(value):
    high = value.astype(BF16).astype(F32)
    mid = (value - high).astype(BF16).astype(F32)
    return high, mid, value - high - mid


def kernel(
    n, rows, heads, lat, pad,
    lengths, blocks, hidden, q_gain, kv_gain,
    q_down, kv_down, q_up, w_uk, cache, w_uv, o_proj,
    out,
    v_qd, v_kd, v_qu, v_uk, v_ca, v_uv, v_op, v_ct,
    s1, r1, g2, qf, qs, qall, s4, r4, s5, r5,
    load_sem, share_sem, send_sem, recv_sem,
):
    me = lax.axis_index("ctx")
    ql = q_down.shape[1]
    kvw = kv_down.shape[1]
    kr = heads * rows
    head_width = NOPE + ROPE
    q_rows = q_up.shape[0]
    o_rows = o_proj.shape[0]
    scale = head_width ** (-0.5)

    loads = []

    def load(src, dst, parts=1):
        mine = []
        size = src.shape[0] // parts
        for part in range(parts):
            where = pl.ds(part * size, size)
            copy = pltpu.make_async_copy(src.at[where], dst.at[where], load_sem.at[len(loads)])
            copy.start()
            loads.append(copy)
            mine.append(copy)
        return mine

    l_qd = load(q_down, v_qd)
    l_kd = load(kv_down, v_kd)
    l_qu = load(q_up, v_qu, 4)
    l_uk = load(w_uk, v_uk)
    spot = lax.rem(me, SHARE)
    l_ca = load(cache, v_ca.at[0])
    l_uv = load(w_uv, v_uv)
    l_op = load(o_proj, v_op, 8)

    def arrive(copies):
        for copy in copies:
            copy.wait()

    everyone = (n, me, lambda index: index)
    alike = (n // SHARE, me // SHARE, lambda index: index * SHARE + spot)

    def remote(phase, src, dst, device):
        return pltpu.make_async_remote_copy(
            src_ref=src, dst_ref=dst, send_sem=send_sem.at[phase], recv_sem=recv_sem.at[phase],
            device_id={"ctx": device}, device_id_type=MESH,
        )

    def around(mine, k, size):
        peer = mine + k
        return jnp.where(peer >= size, peer - size, peer)

    def for_peers(team, body):
        size, mine, _ = team
        if size <= 16:
            for k in range(1, size):
                body(around(mine, k, size))
        else:
            lax.fori_loop(1, size, lambda k, _: (body(around(mine, k, size)), 0)[1], 0)

    barrier = pltpu.get_barrier_semaphore()
    for_peers(everyone, lambda peer: pl.semaphore_signal(
        barrier, inc=1, device_id={"ctx": peer}, device_id_type=MESH
    ))

    def send_all(phase, team, source, dst):
        _, mine, device = team
        for_peers(
            team, lambda peer: remote(phase, source(peer), dst.at[mine], device(peer)).start()
        )

    def whole(phase, team, dst):
        view = dst.at[pl.ds(0, team[0] - 1)]
        return remote(phase, view, view, around(me, 1, n))

    def wait_all(phase, team, dst):
        whole(phase, team, dst).wait_recv()

    q_chunks = ql // LANES
    kv_chunks = -(-kvw // LANES)
    chunks = q_chunks + kv_chunks
    s1[...] = jnp.zeros_like(s1)
    x = hidden[...]
    arrive(l_qd)
    q_part = dot(x, v_qd[...])
    arrive(l_kd)
    kv_part = dot(x, v_kd[...])
    for c in range(chunks):
        d, s = c % n, c // n
        where = pl.ds(s * rows, rows)
        if c < q_chunks:
            s1[d, where, :] = q_part[:, c * LANES:(c + 1) * LANES]
        else:
            begin = (c - q_chunks) * LANES
            width = min(LANES, kvw - begin)
            s1[d, where, :width] = kv_part[:, begin:begin + width]
    r1[me] = s1[me]
    pl.semaphore_wait(barrier, n - 1)
    send_all(0, everyone, lambda peer: s1.at[peer], r1)
    near = me + 1 - 2 * lax.rem(me, 2)
    far = me + 2 - 4 * (spot // 2)

    def share(step, src, slot, device):
        return pltpu.make_async_remote_copy(
            src_ref=src, dst_ref=v_ca.at[slot], send_sem=share_sem.at[step],
            recv_sem=share_sem.at[step + 3], device_id={"ctx": device}, device_id_type=MESH,
        )

    swaps = [share(0, cache, 2, far), share(1, cache, 1, near)]
    for copy in swaps:
        copy.start()

    tokens = cache.shape[2]
    token = lax.broadcasted_iota(jnp.int32, (1, tokens), 1)
    owners = (me, near, far, near + far - me)
    position = jnp.concatenate([owner * tokens + token for owner in owners], axis=1)
    block_of = position // BLOCK
    used = []
    for r in range(rows):
        hit = block_of == blocks[r, 0]
        for k in range(1, blocks.shape[1]):
            hit = hit | (block_of == blocks[r, k])
        used.append(jnp.where(hit & (position < lengths[r]), 1.0, 0.0))
    used = jnp.concatenate(used, axis=1)
    size = n // SHARE
    mine = me // SHARE
    cut = (size + 1) // 2
    shape = (cut * pad, rows * SHARE * tokens)
    row_of_token = lax.broadcasted_iota(jnp.int32, shape, 1) // (SHARE * tokens)
    row_of_query = lax.broadcasted_iota(jnp.int32, shape, 0) % rows
    valid = (row_of_token == row_of_query) & (used > 0.5)
    if pad > kr:
        qs[...] = jnp.zeros_like(qs)

    wait_all(0, everyone, r1)
    g2[me] = jnp.sum(r1[...], axis=0)
    send_all(1, everyone, lambda peer: g2.at[me], g2)
    wait_all(1, everyone, g2)

    def chunk(c):
        return g2[c % n, pl.ds((c // n) * rows, rows), :]

    q_low = jnp.concatenate([chunk(c) for c in range(q_chunks)], axis=1)
    kv_new = jnp.concatenate([chunk(c) for c in range(q_chunks, chunks)], axis=1)[:, :kvw]
    q_mean = jnp.sum(q_low * q_low, axis=1, keepdims=True) * (1.0 / ql)
    gain = jnp.concatenate([q_gain[c:c + 1, :] for c in range(q_chunks)], axis=1)
    q_normed = (q_low * lax.rsqrt(q_mean + 1e-06) * gain).astype(BF16)
    arrive(l_qu)
    qf[...] = dot(q_normed, v_qu[...]).astype(BF16).astype(F32)
    arrive(l_uk)
    for h in range(heads):
        nope = qf[:, h * head_width:h * head_width + NOPE].astype(BF16)
        where = pl.ds(h * rows, rows)
        qs[where, :lat] = dot(nope, v_uk[h])
        qs[where, lat:] = qf[:, h * head_width + NOPE:(h + 1) * head_width]
    query = qs[...].astype(BF16)
    qall[0] = query
    for k in range(1, size):
        device = alike[2](around(mine, k, size))
        remote(2 if k < cut else 3, qall.at[0], qall.at[k], device).start()

    swaps[0].wait_recv()
    swaps.append(share(2, v_ca.at[2], 3, near))
    swaps[2].start()

    kv_lat = kv_new[:, :lat]
    kv_mean = jnp.sum(kv_lat * kv_lat, axis=1, keepdims=True) * (1.0 / lat)
    lat_new = kv_lat * lax.rsqrt(kv_mean + 1e-06) * kv_gain[...]
    key_new = jnp.concatenate([lat_new, kv_new[:, lat:]], axis=1).astype(BF16).astype(F32)
    own_row = lax.broadcasted_iota(jnp.int32, (pad, kvw), 0) % rows
    key_rows = jnp.broadcast_to(key_new[0:1], (pad, kvw))
    for r in range(1, rows):
        key_rows = jnp.where(own_row == r, jnp.broadcast_to(key_new[r:r + 1], (pad, kvw)), key_rows)
    own = scale * jnp.sum(query.astype(F32) * key_rows, axis=1, keepdims=True)

    parts = [(slot, r) for r in range(rows) for slot in range(SHARE)]
    arrive(l_ca)
    for slot in range(SHARE):
        if slot == 1 or slot == 3:
            swaps[1 if slot == 1 else 2].wait_recv()
        for r in range(rows):
            place = parts.index((slot, r))
            v_ct[place * tokens:(place + 1) * tokens, :] = v_ca[slot, r, :lat, :].T

    def arrived(phase, ref, begin, count):
        view = ref.at[pl.ds(begin, count)]
        return remote(phase, view, view, around(me, 1, n))

    stages = [(2, 0, cut), (3, cut, size - cut)]
    for phase, begin, count in stages:
        skip = 1 if begin == 0 else 0
        arrived(phase, qall, begin + skip, count - skip).wait_recv()
        q_mat = qall[begin:begin + count].reshape(count * pad, kvw)
        score = scale * jnp.concatenate([dot(q_mat, v_ca[slot, r]) for slot, r in parts], axis=1)
        here = valid[:count * pad]
        peak = jnp.max(jnp.where(here, score, -1e30), axis=1, keepdims=True)
        expo = jnp.where(here, jnp.exp(score - peak), 0.0)
        total = jnp.sum(expo, axis=1, keepdims=True)
        numer = dot(expo.astype(BF16), v_ct[...])
        s4[begin:begin + count, :, :lat] = numer.astype(BF16).reshape(count, pad, lat)
        lane = lax.broadcasted_iota(jnp.int32, (count * pad, LANES), 1)
        stats = jnp.zeros((count * pad, LANES), F32)
        for place, piece in enumerate(split3(peak) + split3(total)):
            stats = jnp.where(lane == place, piece, stats)
        s4[begin:begin + count, :, lat:] = stats.astype(BF16).reshape(count, pad, LANES)
        for k in range(begin + skip, begin + count):
            device = alike[2](around(mine, size - k, size))
            remote(4, s4.at[k], r4.at[k], device).start()
    r4[0] = s4[0]
    wait_all(4, alike, r4)

    got = r4[:, :, lat:].astype(F32)
    peaks = got[:, :, 0:1] + got[:, :, 1:2] + got[:, :, 2:3]
    totals = got[:, :, 3:4] + got[:, :, 4:5] + got[:, :, 5:6]
    top = jnp.maximum(jnp.max(peaks, axis=0), own)
    factor = jnp.exp(peaks - top[None])
    own_weight = jnp.exp(own - top)
    denom = jnp.sum(totals * factor, axis=0) + own_weight
    mixed = own_weight * key_rows[:, :lat]
    for d in range(n // SHARE):
        mixed = mixed + factor[d] * r4[d, :, :lat].astype(F32)
    latent = (mixed / denom).astype(BF16).astype(F32)
    arrive(l_uv)
    head_out = jnp.concatenate(
        [dot(latent[h * rows:(h + 1) * rows].astype(BF16), v_uv[h]) for h in range(heads)], axis=1
    ).astype(BF16)

    arrive(l_op)
    width = out.shape[1]
    group = math.lcm(width, 2 * LANES)
    for g in range(n * width // group):
        part = dot(head_out, v_op[:, g * group:(g + 1) * group])
        for i in range(group // width):
            d = g * (group // width) + i
            s5[d] = part[:, i * width:(i + 1) * width]

            @pl.when(me != d)
            def _():
                remote(5, s5.at[d], r5.at[me], d).start()

    r5[me] = s5[me]
    wait_all(5, everyone, r5)
    out[...] = jnp.sum(r5[...], axis=0).astype(BF16)
    for phase, team, dst in (
        (0, everyone, r1), (1, everyone, g2), (4, alike, r4), (5, everyone, r5)
    ):
        whole(phase, team, dst).wait_send()
    for copy in swaps:
        copy.wait_send()
    for phase, begin, count in stages:
        skip = 1 if begin == 0 else 0
        arrived(phase, qall, begin + skip, count - skip).wait_send()


def solution(mesh):
    n = mesh.shape["ctx"]

    def per_device(
        hidden, q_down, q_gain, q_up, w_uk, kv_down, kv_gain, w_uv, o_proj, cache, lengths, blocks
    ):
        rows = hidden.shape[0]
        heads, _, lat = w_uk.shape
        kvw = kv_down.shape[1]
        width = o_proj.shape[1] // n
        pad = -(-rows * heads // 16) * 16
        chunks = q_down.shape[1] // LANES + -(-kvw // LANES)
        held = -(-chunks // n) * rows
        vmem = pl.BlockSpec(memory_space=pltpu.VMEM)
        smem = pl.BlockSpec(memory_space=pltpu.SMEM)
        hbm = pl.BlockSpec(memory_space=pl.ANY)
        cache = jnp.swapaxes(cache, 1, 2)
        big = (q_down, kv_down, q_up, w_uk, cache, w_uv, o_proj)
        held_in = [a.shape for a in big]
        held_in[4] = (SHARE,) + cache.shape
        return pl.pallas_call(
            functools.partial(kernel, n, rows, heads, lat, pad),
            out_shape=jax.ShapeDtypeStruct((rows, width), BF16),
            in_specs=[smem, smem, vmem, vmem, vmem] + [hbm] * len(big),
            out_specs=vmem,
            scratch_shapes=[pltpu.VMEM(shape, BF16) for shape in held_in] + [
                pltpu.VMEM((SHARE * rows * cache.shape[2], lat), BF16),
                pltpu.VMEM((n, held, LANES), F32),
                pltpu.VMEM((n, held, LANES), F32),
                pltpu.VMEM((n, held, LANES), F32),
                pltpu.VMEM((rows, q_up.shape[1]), F32),
                pltpu.VMEM((pad, kvw), F32),
                pltpu.VMEM((n // SHARE, pad, kvw), BF16),
                pltpu.VMEM((n // SHARE, pad, lat + LANES), BF16),
                pltpu.VMEM((n // SHARE, pad, lat + LANES), BF16),
                pltpu.VMEM((n, rows, width), F32),
                pltpu.VMEM((n, rows, width), F32),
                pltpu.SemaphoreType.DMA((17,)),
                pltpu.SemaphoreType.DMA((6,)),
                pltpu.SemaphoreType.DMA((6,)),
                pltpu.SemaphoreType.DMA((6,)),
            ],
            compiler_params=pltpu.CompilerParams(
                collective_id=0, has_side_effects=True, vmem_limit_bytes=56 * 1024 * 1024
            ),
        )(lengths, blocks, hidden, q_gain.reshape(-1, LANES), kv_gain[None], *big)

    placed = (
        P("grp", "ctx"),
        P("ctx", None),
        P(),
        P(None, "ctx"),
        P("ctx", None, None),
        P("ctx", None),
        P(),
        P("ctx", None, None),
        P("ctx", None),
        P("grp", "ctx", None),
        P("grp"),
        P("grp", None),
    )
    return jax.shard_map(
        per_device, mesh=mesh, in_specs=placed, out_specs=P("grp", "ctx"), check_vma=False
    )
```

```python
import functools
import math

import jax
import jax.numpy as jnp
from jax import lax
from jax.experimental import pallas as pl
from jax.experimental.pallas import tpu as pltpu
from jax.sharding import PartitionSpec as P

NOPE = 128
ROPE = 64
PAIR = 2
BLOCK = 64
LANES = 128
F32 = jnp.float32
BF16 = jnp.bfloat16
MESH = pl.DeviceIdType.MESH


def dot(a, b):
    return jnp.dot(a, b, preferred_element_type=F32)


def split3(value):
    high = value.astype(BF16).astype(F32)
    mid = (value - high).astype(BF16).astype(F32)
    return high, mid, value - high - mid


def kernel(
    n, rows, heads, lat, pad,
    lengths, blocks, hidden, q_gain, kv_gain,
    q_down, kv_down, q_up, w_uk, cache, w_uv, o_proj,
    out,
    v_qd, v_kd, v_qu, v_uk, v_ca, v_uv, v_op, v_ct,
    s1, r1, g2, qf, qs, qall, s4, r4, s5, r5,
    load_sem, pair_sem, send_sem, recv_sem,
):
    me = lax.axis_index("ctx")
    ql = q_down.shape[1]
    kvw = kv_down.shape[1]
    kr = heads * rows
    head_width = NOPE + ROPE
    q_rows = q_up.shape[0]
    o_rows = o_proj.shape[0]
    scale = head_width ** (-0.5)

    loads = []

    def load(src, dst, parts=1):
        mine = []
        size = src.shape[0] // parts
        for part in range(parts):
            where = pl.ds(part * size, size)
            copy = pltpu.make_async_copy(src.at[where], dst.at[where], load_sem.at[len(loads)])
            copy.start()
            loads.append(copy)
            mine.append(copy)
        return mine

    l_qd = load(q_down, v_qd)
    l_kd = load(kv_down, v_kd)
    l_qu = load(q_up, v_qu, 4)
    l_uk = load(w_uk, v_uk)
    core = lax.rem(me, PAIR)
    l_ca = load(cache, v_ca.at[core])
    l_uv = load(w_uv, v_uv)
    l_op = load(o_proj, v_op, 8)

    def arrive(copies):
        for copy in copies:
            copy.wait()

    everyone = (n, me, lambda index: index)
    alike = (n // PAIR, me // PAIR, lambda index: index * PAIR + core)

    def remote(phase, src, dst, device):
        return pltpu.make_async_remote_copy(
            src_ref=src, dst_ref=dst, send_sem=send_sem.at[phase], recv_sem=recv_sem.at[phase],
            device_id={"ctx": device}, device_id_type=MESH,
        )

    def around(mine, k, size):
        peer = mine + k
        return jnp.where(peer >= size, peer - size, peer)

    def for_peers(team, body):
        size, mine, _ = team
        if size <= 16:
            for k in range(1, size):
                body(around(mine, k, size))
        else:
            lax.fori_loop(1, size, lambda k, _: (body(around(mine, k, size)), 0)[1], 0)

    barrier = pltpu.get_barrier_semaphore()
    for_peers(everyone, lambda peer: pl.semaphore_signal(
        barrier, inc=1, device_id={"ctx": peer}, device_id_type=MESH
    ))

    def send_all(phase, team, source, dst):
        _, mine, device = team
        for_peers(
            team, lambda peer: remote(phase, source(peer), dst.at[mine], device(peer)).start()
        )

    def whole(phase, team, dst):
        view = dst.at[pl.ds(0, team[0] - 1)]
        return remote(phase, view, view, around(me, 1, n))

    def wait_all(phase, team, dst):
        whole(phase, team, dst).wait_recv()

    q_chunks = ql // LANES
    kv_chunks = -(-kvw // LANES)
    chunks = q_chunks + kv_chunks
    s1[...] = jnp.zeros_like(s1)
    x = hidden[...]
    arrive(l_qd)
    q_part = dot(x, v_qd[...])
    arrive(l_kd)
    kv_part = dot(x, v_kd[...])
    for c in range(chunks):
        d, s = c % n, c // n
        where = pl.ds(s * rows, rows)
        if c < q_chunks:
            s1[d, where, :] = q_part[:, c * LANES:(c + 1) * LANES]
        else:
            begin = (c - q_chunks) * LANES
            width = min(LANES, kvw - begin)
            s1[d, where, :width] = kv_part[:, begin:begin + width]
    r1[me] = s1[me]
    pl.semaphore_wait(barrier, n - 1)
    send_all(0, everyone, lambda peer: s1.at[peer], r1)
    partner = me + 1 - 2 * core
    share = pltpu.make_async_remote_copy(
        src_ref=cache, dst_ref=v_ca.at[core], send_sem=pair_sem.at[0], recv_sem=pair_sem.at[1],
        device_id={"ctx": partner}, device_id_type=MESH,
    )
    share.start()

    tokens = cache.shape[2]
    token = lax.broadcasted_iota(jnp.int32, (1, PAIR * tokens), 1)
    position = (me - core) * tokens + token
    block_of = position // BLOCK
    used = []
    for r in range(rows):
        hit = block_of == blocks[r, 0]
        for k in range(1, blocks.shape[1]):
            hit = hit | (block_of == blocks[r, k])
        used.append(jnp.where(hit & (position < lengths[r]), 1.0, 0.0))
    used = jnp.concatenate(used, axis=1)
    size = n // PAIR
    mine = me // PAIR
    cut = (size + 1) // 2
    shape = (cut * pad, rows * PAIR * tokens)
    row_of_token = lax.broadcasted_iota(jnp.int32, shape, 1) // (PAIR * tokens)
    row_of_query = lax.broadcasted_iota(jnp.int32, shape, 0) % rows
    valid = (row_of_token == row_of_query) & (used > 0.5)
    if pad > kr:
        qs[...] = jnp.zeros_like(qs)

    wait_all(0, everyone, r1)
    g2[me] = jnp.sum(r1[...], axis=0)
    send_all(1, everyone, lambda peer: g2.at[me], g2)
    wait_all(1, everyone, g2)

    def chunk(c):
        return g2[c % n, pl.ds((c // n) * rows, rows), :]

    q_low = jnp.concatenate([chunk(c) for c in range(q_chunks)], axis=1)
    kv_new = jnp.concatenate([chunk(c) for c in range(q_chunks, chunks)], axis=1)[:, :kvw]
    q_mean = jnp.sum(q_low * q_low, axis=1, keepdims=True) * (1.0 / ql)
    gain = jnp.concatenate([q_gain[c:c + 1, :] for c in range(q_chunks)], axis=1)
    q_normed = (q_low * lax.rsqrt(q_mean + 1e-06) * gain).astype(BF16)
    arrive(l_qu)
    qf[...] = dot(q_normed, v_qu[...]).astype(BF16).astype(F32)
    arrive(l_uk)
    for h in range(heads):
        nope = qf[:, h * head_width:h * head_width + NOPE].astype(BF16)
        where = pl.ds(h * rows, rows)
        qs[where, :lat] = dot(nope, v_uk[h])
        qs[where, lat:] = qf[:, h * head_width + NOPE:(h + 1) * head_width]
    query = qs[...].astype(BF16)
    qall[0] = query
    for k in range(1, size):
        device = alike[2](around(mine, k, size))
        remote(2 if k < cut else 3, qall.at[0], qall.at[k], device).start()

    kv_lat = kv_new[:, :lat]
    kv_mean = jnp.sum(kv_lat * kv_lat, axis=1, keepdims=True) * (1.0 / lat)
    lat_new = kv_lat * lax.rsqrt(kv_mean + 1e-06) * kv_gain[...]
    key_new = jnp.concatenate([lat_new, kv_new[:, lat:]], axis=1).astype(BF16).astype(F32)
    own_row = lax.broadcasted_iota(jnp.int32, (pad, kvw), 0) % rows
    key_rows = jnp.broadcast_to(key_new[0:1], (pad, kvw))
    for r in range(1, rows):
        key_rows = jnp.where(own_row == r, jnp.broadcast_to(key_new[r:r + 1], (pad, kvw)), key_rows)
    own = scale * jnp.sum(query.astype(F32) * key_rows, axis=1, keepdims=True)

    arrive(l_ca)
    pltpu.make_async_remote_copy(
        src_ref=cache, dst_ref=v_ca.at[1 - core], send_sem=pair_sem.at[0], recv_sem=pair_sem.at[1],
        device_id={"ctx": partner}, device_id_type=MESH,
    ).wait()
    parts = [(half, r) for r in range(rows) for half in range(PAIR)]
    for place, (half, r) in enumerate(parts):
        v_ct[place * tokens:(place + 1) * tokens, :] = v_ca[half, r, :lat, :].T

    def arrived(phase, ref, begin, count):
        view = ref.at[pl.ds(begin, count)]
        return remote(phase, view, view, around(me, 1, n))

    stages = [(2, 0, cut), (3, cut, size - cut)]
    for phase, begin, count in stages:
        skip = 1 if begin == 0 else 0
        arrived(phase, qall, begin + skip, count - skip).wait_recv()
        q_mat = qall[begin:begin + count].reshape(count * pad, kvw)
        score = scale * jnp.concatenate([dot(q_mat, v_ca[half, r]) for half, r in parts], axis=1)
        here = valid[:count * pad]
        peak = jnp.max(jnp.where(here, score, -1e30), axis=1, keepdims=True)
        expo = jnp.where(here, jnp.exp(score - peak), 0.0)
        total = jnp.sum(expo, axis=1, keepdims=True)
        numer = dot(expo.astype(BF16), v_ct[...])
        s4[begin:begin + count, :, :lat] = numer.astype(BF16).reshape(count, pad, lat)
        lane = lax.broadcasted_iota(jnp.int32, (count * pad, LANES), 1)
        stats = jnp.zeros((count * pad, LANES), F32)
        for place, piece in enumerate(split3(peak) + split3(total)):
            stats = jnp.where(lane == place, piece, stats)
        s4[begin:begin + count, :, lat:] = stats.astype(BF16).reshape(count, pad, LANES)
        for k in range(begin + skip, begin + count):
            device = alike[2](around(mine, size - k, size))
            remote(4, s4.at[k], r4.at[k], device).start()
    r4[0] = s4[0]
    wait_all(4, alike, r4)

    got = r4[:, :, lat:].astype(F32)
    peaks = got[:, :, 0:1] + got[:, :, 1:2] + got[:, :, 2:3]
    totals = got[:, :, 3:4] + got[:, :, 4:5] + got[:, :, 5:6]
    top = jnp.maximum(jnp.max(peaks, axis=0), own)
    factor = jnp.exp(peaks - top[None])
    own_weight = jnp.exp(own - top)
    denom = jnp.sum(totals * factor, axis=0) + own_weight
    mixed = own_weight * key_rows[:, :lat]
    for d in range(n // PAIR):
        mixed = mixed + factor[d] * r4[d, :, :lat].astype(F32)
    latent = (mixed / denom).astype(BF16).astype(F32)
    arrive(l_uv)
    head_out = jnp.concatenate(
        [dot(latent[h * rows:(h + 1) * rows].astype(BF16), v_uv[h]) for h in range(heads)], axis=1
    ).astype(BF16)

    arrive(l_op)
    width = out.shape[1]
    group = math.lcm(width, 2 * LANES)
    per = group // width
    groups = n // per
    home = me // per
    seat = me - home * per
    for off in sorted(range(groups), key=lambda off: -min(off, groups - off)):
        g = around(home, off, groups)
        part = dot(head_out, v_op[:, pl.ds(pl.multiple_of(g * group, 2 * LANES), group)])
        for i in range(per):
            s5[g * per + i] = part[:, i * width:(i + 1) * width]
        for i in range(0 if off else 1, per):
            d = g * per + (i if off else around(seat, i, per))
            remote(5, s5.at[d], r5.at[me], d).start()

    r5[me] = s5[me]
    wait_all(5, everyone, r5)
    out[...] = jnp.sum(r5[...], axis=0).astype(BF16)
    for phase, team, dst in (
        (0, everyone, r1), (1, everyone, g2), (4, alike, r4), (5, everyone, r5)
    ):
        whole(phase, team, dst).wait_send()
    for phase, begin, count in stages:
        skip = 1 if begin == 0 else 0
        arrived(phase, qall, begin + skip, count - skip).wait_send()


def solution(mesh):
    n = mesh.shape["ctx"]

    def per_device(
        hidden, q_down, q_gain, q_up, w_uk, kv_down, kv_gain, w_uv, o_proj, cache, lengths, blocks
    ):
        rows = hidden.shape[0]
        heads, _, lat = w_uk.shape
        kvw = kv_down.shape[1]
        width = o_proj.shape[1] // n
        pad = -(-rows * heads // 16) * 16
        chunks = q_down.shape[1] // LANES + -(-kvw // LANES)
        held = -(-chunks // n) * rows
        vmem = pl.BlockSpec(memory_space=pltpu.VMEM)
        smem = pl.BlockSpec(memory_space=pltpu.SMEM)
        hbm = pl.BlockSpec(memory_space=pl.ANY)
        cache = jnp.swapaxes(cache, 1, 2)
        big = (q_down, kv_down, q_up, w_uk, cache, w_uv, o_proj)
        held_in = [a.shape for a in big]
        held_in[4] = (PAIR,) + cache.shape
        return pl.pallas_call(
            functools.partial(kernel, n, rows, heads, lat, pad),
            out_shape=jax.ShapeDtypeStruct((rows, width), BF16),
            in_specs=[smem, smem, vmem, vmem, vmem] + [hbm] * len(big),
            out_specs=vmem,
            scratch_shapes=[pltpu.VMEM(shape, BF16) for shape in held_in] + [
                pltpu.VMEM((PAIR * rows * cache.shape[2], lat), BF16),
                pltpu.VMEM((n, held, LANES), F32),
                pltpu.VMEM((n, held, LANES), F32),
                pltpu.VMEM((n, held, LANES), F32),
                pltpu.VMEM((rows, q_up.shape[1]), F32),
                pltpu.VMEM((pad, kvw), F32),
                pltpu.VMEM((n // PAIR, pad, kvw), BF16),
                pltpu.VMEM((n // PAIR, pad, lat + LANES), BF16),
                pltpu.VMEM((n // PAIR, pad, lat + LANES), BF16),
                pltpu.VMEM((n, rows, width), F32),
                pltpu.VMEM((n, rows, width), F32),
                pltpu.SemaphoreType.DMA((17,)),
                pltpu.SemaphoreType.DMA((2,)),
                pltpu.SemaphoreType.DMA((6,)),
                pltpu.SemaphoreType.DMA((6,)),
            ],
            compiler_params=pltpu.CompilerParams(
                collective_id=0, has_side_effects=True, vmem_limit_bytes=56 * 1024 * 1024
            ),
        )(lengths, blocks, hidden, q_gain.reshape(-1, LANES), kv_gain[None], *big)

    placed = (
        P("grp", "ctx"),
        P("ctx", None),
        P(),
        P(None, "ctx"),
        P("ctx", None, None),
        P("ctx", None),
        P(),
        P("ctx", None, None),
        P("ctx", None),
        P("grp", "ctx", None),
        P("grp"),
        P("grp", None),
    )
    return jax.shard_map(
        per_device, mesh=mesh, in_specs=placed, out_specs=P("grp", "ctx"), check_vma=False
    )
```
